512 devices in a mesh: ctx: 32 (over z, core), pb: 16 (over y, x).
Axes of the slice: x: 4, y: 4, z: 16, core: 2. Of those that a mesh axis runs over, the one named last changes fastest.
Arguments:
- q_latent: bfloat16 [1024, 73728], P(('ctx', 'pb')), may hold values from -80 to 80
- kv_cache: bfloat16 [16384, 576], P('ctx'), may hold values from -6 to 6
- index_queries: bfloat16 [1024, 8192], P(('ctx', 'pb')), may hold values from -6 to 6
- index_weights: bfloat16 [1024, 64], P(('ctx', 'pb')), may hold values from -0.75 to 0.75
- index_keys: bfloat16 [16384, 128], P(('ctx', 'pb')), may hold values from -6 to 6
- q_blocks: int32 [1024, 32], P(('ctx', 'pb')), may hold values from 0 to 255, as said below
Outputs:
- attention: bfloat16 [1024, 65536], P(('ctx', 'pb'))
- index_scores: bfloat16 [1024, 16384], P(('ctx', 'pb'))
The draws below stay inside these ranges and needn't reach their ends.
Inputs may be any that keep to these rules, and one draw needn't show every extreme that they name: `q_blocks`: each row names 32 different blocks, none after the block that holds pos of that row, and names both that block and block 0. Over the rows of one device (2 rows in a row of the ctx+pb order) at most 2 different named blocks lie in one context shard of 512 keys; every device names exactly 2 blocks of shard 0.
All inputs are finite; a program needn't handle non-finite values.
Results may differ from the reference program's by a relative error of at most 0.0037.
Values may be sent and summed in bfloat16 or wider, within the bound.
No kernel may reach another device: no remote copies, remote signals or barrier semaphores. Data moves between devices by JAX's collectives and lax.ppermute only.
A program may use at most 64 MiB of HBM per device.

```python
import jax
import jax.numpy as jnp
from jax import lax

H = 128
DL = 512
DQK = 576
IH = 64
ID = 128
BLK = 64
TOPB = 32
CTX_DEV = 512
Q_DEV = 2
CONTEXT = 16384
QUERIES = 1024
CAP = 2


def cache_values(key):
    return jnp.clip(jax.random.normal(key, (CONTEXT, DQK), jnp.float32), -6.0, 6.0)


def draw_kv_cache(key, part):
    values = cache_values(key)
    return values.astype(jnp.bfloat16)


def draw_q_latent(key, part):
    key = jax.random.fold_in(key, 5)
    normal_part = 0.5 * jnp.clip(jax.random.normal(key, (QUERIES, H, DQK), jnp.float32), -6.0, 6.0)
    values = normal_part
    values = jnp.clip(values, -80.0, 80.0)
    return values.reshape(QUERIES, H * DQK).astype(jnp.bfloat16)


def draw_q_blocks(key, part):
    key = jax.random.fold_in(key, 7)
    pool_key, pick_key, order_key = jax.random.split(key, 3)
    shard_blocks = CTX_DEV // BLK
    shard_count = CONTEXT // CTX_DEV
    group_count = QUERIES // Q_DEV
    first_block = (CONTEXT - QUERIES + jnp.arange(group_count, dtype=jnp.int32) * Q_DEV) // BLK
    own_shard = (first_block // shard_blocks)[:, None, None]
    own_offset = (first_block % shard_blocks)[:, None, None]
    shard_ids = jnp.arange(shard_count, dtype=jnp.int32)[None, :, None]
    offsets = jnp.arange(shard_blocks, dtype=jnp.int32)[None, None, :]
    ceiling = 1 << 26
    priority = jax.random.randint(pool_key, (group_count, shard_count, shard_blocks), 0, 1 << 16, dtype=jnp.int32) * shard_blocks + offsets
    priority = jnp.where((shard_ids == 0) & (offsets == 0), ceiling, priority)
    priority = jnp.where((shard_ids == own_shard) & (offsets == own_offset), ceiling, priority)
    priority = jnp.where((shard_ids == own_shard) & (offsets > own_offset), -1, priority)
    priority = jnp.where(shard_ids > own_shard, -1, priority)
    ranked, picked = lax.top_k(priority, CAP)
    pool_blocks = shard_ids * shard_blocks + picked
    pool_valid = ranked >= 0
    forced = pool_valid & ((shard_ids == 0) | (shard_ids == own_shard))
    pool_width = shard_count * CAP
    member = jnp.arange(QUERIES, dtype=jnp.int32) // Q_DEV
    pool_rows = pool_blocks.reshape(group_count, pool_width)[member]
    valid_rows = pool_valid.reshape(group_count, pool_width)[member]
    forced_rows = forced.reshape(group_count, pool_width)[member]
    jitter = jax.random.randint(pick_key, (QUERIES, pool_width), 0, 1 << 16, dtype=jnp.int32) * pool_width + jnp.arange(pool_width, dtype=jnp.int32)[None, :]
    pick_priority = jnp.where(forced_rows, 1 << 28, jnp.where(valid_rows, jitter, -1))
    taken_values, taken = lax.top_k(pick_priority, TOPB)
    selected = jnp.take_along_axis(pool_rows, taken, axis=1)
    shuffle = jax.random.randint(order_key, (QUERIES, TOPB), 0, 1 << 16, dtype=jnp.int32) * TOPB + jnp.arange(TOPB, dtype=jnp.int32)[None, :]
    ordering = jnp.argsort(shuffle, axis=1)
    return jnp.take_along_axis(selected, ordering, axis=1).astype(jnp.int32)


def steps_of(own_key, dims, pieces, least, largest):
    factor_of = 1.0
    for dim, blocks in pieces:
        draws = jax.random.uniform(jax.random.fold_in(jax.random.fold_in(own_key, 6), dim), (blocks,), jnp.float32, least / len(pieces), largest / len(pieces))
        factor_of = factor_of * jnp.repeat(jnp.exp(draws), dims[dim] // blocks).reshape((-1,) + (1,) * (len(dims) - 1 - dim))
    return factor_of


def normal_values(rng, shape, deviation, reach, cuts=(), kind=jnp.bfloat16):
    level = steps_of(rng, shape, cuts, -0.22, 0.18) if cuts else 1.0
    result = jax.random.normal(rng, shape, jnp.float32) * deviation * level
    return jnp.minimum(jnp.maximum(result, -reach), reach).astype(kind)


def setup_inputs(seed: int = 0) -> dict:
    arg_keys = jax.random.split(jax.random.key(seed), 7)
    q_latent = draw_q_latent(jax.random.fold_in(arg_keys[6], 71), 0)
    kv_cache = draw_kv_cache(jax.random.fold_in(arg_keys[6], 71), 0)
    index_queries = normal_values(arg_keys[2], (QUERIES, IH * ID), 1.0, 6.0, ((0, 512),))
    index_weights = normal_values(arg_keys[3], (QUERIES, IH), IH ** -0.5, 0.75, ((0, 512),))
    index_keys = normal_values(arg_keys[4], (CONTEXT, ID), 1.0, 6.0, ((0, 512),))
    q_blocks = draw_q_blocks(jax.random.fold_in(arg_keys[6], 71), 0)
    return dict(q_latent=q_latent, kv_cache=kv_cache, index_queries=index_queries, index_weights=index_weights, index_keys=index_keys, q_blocks=q_blocks)


score_scale = 192.0 ** -0.5


def reference(q_latent, kv_cache, index_queries, index_weights, index_keys, q_blocks):
    def index_row(row_pair):
        query_row, weight_row = row_pair
        products = jnp.dot(query_row.reshape(IH, ID), index_keys.T, preferred_element_type=jnp.float32)
        active = jnp.maximum(products * (ID ** -0.5), 0.0)
        return jnp.sum(active * weight_row.astype(jnp.float32)[:, None], axis=0).astype(jnp.bfloat16)

    index_scores = lax.map(index_row, (index_queries, index_weights))
    cache_blocks = kv_cache.reshape(CONTEXT // BLK, BLK, DQK)
    positions = jnp.arange(QUERIES, dtype=jnp.int32) + (CONTEXT - QUERIES)

    def attend_row(row_triple):
        query_row, block_row, position = row_triple
        key_rows = cache_blocks[block_row].reshape(TOPB * BLK, DQK)
        key_positions = (block_row[:, None] * BLK + jnp.arange(BLK, dtype=jnp.int32)[None, :]).reshape(TOPB * BLK)
        scores = jnp.dot(query_row.reshape(H, DQK), key_rows.T, preferred_element_type=jnp.float32) * score_scale
        masked = jnp.where(key_positions[None, :] <= position, scores, -1e30)
        highest = jnp.max(masked, axis=1, keepdims=True)
        weights = jnp.exp(masked - highest)
        rounded = (weights / jnp.sum(weights, axis=1, keepdims=True)).astype(jnp.bfloat16)
        attended = jnp.dot(rounded, key_rows[:, :DL], preferred_element_type=jnp.float32)
        return attended.astype(jnp.bfloat16).reshape(H * DL)

    attention = lax.map(attend_row, (q_latent, q_blocks, positions))
    return attention, index_scores
```

```python
import jax
import jax.numpy as jnp
from jax import lax
from jax.experimental import pallas as pl
from jax.experimental.pallas import tpu as pltpu
from jax.sharding import PartitionSpec as P

DL = 512
DQK = 576
ROT = DQK - DL
BLK = 64
IH = 64
ID = 128
HEADS = 128
PLANE = 16
LEVELS = 16
PIECE = BLK // PLANE
KV_COLS = PIECE * DQK
Z_COLS = KV_COLS + 4 * ID
SENT_COLS = KV_COLS + 128
VMEM_LIMIT = 40 * 1024 * 1024

score_scale = 192.0 ** (-0.5)
index_scale = 128.0 ** (-0.5)
f32 = jnp.float32
bf16 = jnp.bfloat16

NEAR = (0, 64, 16)
FAR = (64, 192, 48)


def params():
    return pltpu.CompilerParams(vmem_limit_bytes=VMEM_LIMIT)


def whole():
    return pl.BlockSpec(memory_space=pltpu.VMEM)


def anywhere():
    return pl.BlockSpec(memory_space=pl.ANY)


def iota(shape, dim):
    return lax.broadcasted_iota(jnp.int32, shape, dim)


def table_row(block):
    at = lax.axis_index("ctx")
    half = (block // 8 + at) % 2
    turn = (block // 16 - at // 2 + LEVELS) % 4
    order = jnp.where(turn == 3, 2, jnp.where(turn == 2, 3, turn))
    inner = block // 64 * 8 + block % 8
    return jnp.where(
        order == 0, half * 32 + inner, 64 + half * 96 + (order - 1) * 32 + inner
    )


def pack_kernel(kv_ref, ik_ref, iq_ref, iw_ref, qb_ref, z_ref, y_ref, keys, rows):
    piece = lax.axis_index("pb")
    shard_keys = kv_ref.shape[1]
    line = iota((PIECE * 8, shard_keys), 0)
    source = (line % 8) * BLK + piece * PIECE + line // 8
    select = jnp.where(source == iota(source.shape, 1), 1.0, 0.0).astype(bf16)
    part = lax.dot_general(
        select, kv_ref[...], (((1,), (1,)), ((), ())), preferred_element_type=f32
    )
    keys[...] = ik_ref[...].astype(f32)
    columns = [part[r * 8 : (r + 1) * 8, :DL] for r in range(PIECE)]
    columns += [part[r * 8 : (r + 1) * 8, DL:] for r in range(PIECE)]
    columns += [keys[pl.ds(j, 8, stride=4), :] for j in range(4)]
    chunk = jnp.concatenate(columns, axis=1).astype(bf16)
    for n in range(4):
        z_ref[n] = chunk
    for h in range(IH):
        rows[pl.ds(h, 2, stride=IH), :] = iq_ref[:, h * ID : (h + 1) * ID].astype(f32)
    weights = iw_ref[...].astype(f32)
    weights = jnp.concatenate([weights[0:1], weights[1:2]], axis=1)
    ids = qb_ref[...].astype(f32)
    ids = jnp.concatenate([ids[0:1], ids[1:2], jnp.zeros((1, 64), f32)], axis=1)
    at = iota((16, 128), 0)
    tail = jnp.where(at == 0, weights, jnp.where(at == 1, ids, 0.0)).astype(bf16)
    head = rows[...].astype(bf16)
    for p in range(PLANE):
        y_ref[p, 0 : 2 * IH, :] = head
        y_ref[p, 2 * IH : 2 * IH + 16, :] = tail


def pack(kv_turned, index_keys, index_queries, index_weights, q_blocks):
    return pl.pallas_call(
        pack_kernel,
        out_shape=(
            jax.ShapeDtypeStruct((4, 8, Z_COLS), bf16),
            jax.ShapeDtypeStruct((PLANE, 2 * IH + 16, ID), bf16),
        ),
        in_specs=[whole()] * 5,
        out_specs=(whole(), whole()),
        scratch_shapes=[pltpu.VMEM((32, ID), f32), pltpu.VMEM((2 * IH, ID), f32)],
        compiler_params=params(),
        name="pack",
    )(kv_turned, index_keys, index_queries, index_weights, q_blocks)


def named_columns(span, ids):
    first, count, unused = span
    lane = iota((count, 128), 1)
    named = jnp.zeros((count, 128), f32)
    for n, row in enumerate(ids):
        place = table_row(row) - first
        hit = jnp.where(place == iota((count, row.shape[1]), 0), 1.0, 0.0)
        named = jnp.where(lane == n, jnp.max(hit, axis=1, keepdims=True), named)
    return named


def slot_codes(span, named):
    count = span[1]
    t, u = iota((count, count), 0), iota((count, count), 1)
    before = jnp.where((t // 8 == u // 8) & (u < t), 1.0, 0.0).astype(bf16)
    rank = jnp.dot(before, named.astype(bf16), preferred_element_type=f32)
    return jnp.where(named > 0.5, rank, -1.0)


def gather_kernel(span, tables, y_ref, scores_ref, out_ref, onehot):
    first, count, slots = span
    rows = [
        y_ref[p, 2 * IH : 2 * IH + 16, :].astype(f32)[1:2, :64].astype(jnp.int32)
        for p in range(PLANE)
    ]
    named = named_columns(span, rows)
    code = slot_codes(span, named)
    width = PLANE * slots
    line, lane = iota((count, width), 0), iota((count, width), 1)
    wide = jnp.full((count, width), -1.0, f32)
    for p in range(PLANE):
        wide = jnp.where(lane // slots == p, code[:, p : p + 1], wide)
    slot = lane % slots
    turned = jnp.where(
        (line // 8 == slot // 2) & (wide == (slot % 2).astype(f32)), 1.0, 0.0
    )
    pad = -count % 128
    turned = jnp.concatenate([turned, jnp.zeros((pad, width), f32)], axis=0)
    onehot[...] = turned.T[:, :count].astype(bf16)
    for c in range(KV_COLS // 256):
        cols = slice(c * 256, (c + 1) * 256)
        rows = jnp.concatenate([ref[:, cols] for ref in tables], axis=0)
        out_ref[:, cols] = jnp.dot(
            onehot[...], rows, preferred_element_type=f32
        ).astype(bf16)
    if scores_ref is not None:
        for p in range(PLANE):
            at = p * slots
            out_ref[at : at + 16, KV_COLS:] = scores_ref[p]
            out_ref[at + 16 : at + slots, KV_COLS:] = jnp.zeros((slots - 16, 128), bf16)


def gather(name, span, tables, y, scores=None):
    first, count, slots = span

    def body(*refs):
        refs = list(refs)
        held = [refs.pop(0) for table in tables]
        y_ref = refs.pop(0)
        scores_ref = None if scores is None else refs.pop(0)
        gather_kernel(span, held, y_ref, scores_ref, *refs)

    operands = [*tables, y] + ([] if scores is None else [scores])
    columns = KV_COLS if scores is None else SENT_COLS
    return pl.pallas_call(
        body,
        out_shape=jax.ShapeDtypeStruct((PLANE * slots, columns), bf16),
        in_specs=[whole()] * len(operands),
        out_specs=whole(),
        scratch_shapes=[pltpu.VMEM((PLANE * slots, count), bf16)],
        compiler_params=params(),
        cost_estimate=pl.CostEstimate(
            flops=2 * PLANE * slots * count * KV_COLS,
            bytes_accessed=3_000_000,
            transcendentals=0,
        ),
        name=name,
    )(*operands)


def score_kernel(*refs):
    tables, y_ref, out_ref, keys = refs[:8], refs[8], refs[9], refs[10]
    tail = jnp.concatenate(
        [y_ref[p, 2 * IH : 2 * IH + 16, :].astype(f32)[0:1] for p in range(PLANE)], axis=0
    )
    weights = jnp.concatenate(
        [tail * index_scale, jnp.zeros((128 - PLANE, 128), f32)], axis=0
    ).T
    lane = iota((128, 128), 1)
    at = lax.axis_index("ctx")
    for n, ref in enumerate(tables):
        step = (0, 1, 3, 2)[n % 4]
        inner = (at // 2 + step) % 4
        core = (at + n // 4) % 2
        for outer in range(4):
            shard = (outer * 4 + inner) * 2 + core
            for j in range(4):
                cols = slice(KV_COLS + j * ID, KV_COLS + (j + 1) * ID)
                keys[pl.ds(shard * 32 + j, 8, stride=4), :] = ref[
                    outer * 8 : (outer + 1) * 8, cols
                ].astype(f32)
    key_rows = keys[...].astype(bf16)

    def peer(p, carry):
        products = lax.dot_general(
            y_ref[p, 0 : 2 * IH, :],
            key_rows,
            (((1,), (1,)), ((), ())),
            preferred_element_type=f32,
        )
        weight = jnp.sum(jnp.where(lane == p, weights, 0.0), axis=1, keepdims=True)
        active = jnp.maximum(products, 0.0) * weight
        lines = []
        for i in range(2):
            total = jnp.sum(active[i * IH : (i + 1) * IH], axis=0, keepdims=True)
            lines += [total[:, c * 128 : (c + 1) * 128] for c in range(8)]
        out_ref[p] = jnp.concatenate(lines, axis=0).astype(bf16)
        return carry

    lax.fori_loop(0, PLANE, peer, 0)


def score(tables, y):
    return pl.pallas_call(
        score_kernel,
        out_shape=jax.ShapeDtypeStruct((PLANE, 16, 128), bf16),
        in_specs=[whole()] * 9,
        out_specs=whole(),
        scratch_shapes=[pltpu.VMEM((1024, ID), f32)],
        compiler_params=params(),
        cost_estimate=pl.CostEstimate(
            flops=2 * 2048 * 128 * 1024, bytes_accessed=2_000_000, transcendentals=0
        ),
        name="score",
    )(*tables, y)


def attend_kernel(q_ref, ids_ref, near_ref, far_ref, out_ref, scores, total):
    rank = lax.axis_index("ctx") * PLANE + lax.axis_index("pb")
    ids = ids_ref[...]
    own_row = table_row(240 + rank * 2 // BLK)
    query = jnp.concatenate([q_ref[0], q_ref[1]], axis=0)
    latent = query[:, :DL]
    rotary = query[:, DL:]
    nothing = jnp.zeros_like(rotary)
    padded = (
        jnp.concatenate([rotary, nothing], axis=1),
        jnp.concatenate([nothing, rotary], axis=1),
    )
    contract = (((1,), (1,)), ((), ()))
    sets = []
    for span, ref in ((NEAR, near_ref), (FAR, far_ref)):
        first, count, slots = span
        one, two = named_columns(span, [ids[0:1]]), named_columns(span, [ids[1:2]])
        members = (one[:, 0:1], two[:, 0:1])
        code = slot_codes(span, jnp.maximum(one, two))[:, 0:1]
        width = PLANE * slots
        line, slot = iota((count, width), 0), iota((count, width), 1) % slots
        onehot = (line // 8 == slot // 2) & (code == (slot % 2).astype(f32))
        limits = []
        for i in range(2):
            offset = ((rank * 2 + i) % BLK).astype(f32)
            limit = jnp.where(line[:, 0:1] + first == own_row, offset, 63.0) + 1.0
            limit = jnp.where(members[i] > 0.5, limit, 0.0)
            limits.append(jnp.sum(jnp.where(onehot, limit, 0.0), axis=0, keepdims=True))
        place = iota((1, width), 1) // slots * PIECE
        for k in range(width // 256):
            rows = slice(k * 256, (k + 1) * 256)
            for r in range(PIECE):
                turn = PIECE * DL + r // 2 * 128
                block = lax.dot_general(
                    latent, ref[rows, r * DL : (r + 1) * DL], contract,
                    preferred_element_type=f32,
                ) + lax.dot_general(
                    padded[r % 2], ref[rows, turn : turn + 128], contract,
                    preferred_element_type=f32,
                )
                at = len(sets) * 256
                sets.append((ref, rows, slice(r * DL, (r + 1) * DL)))
                here = (place[:, rows] + r).astype(f32)
                for i in range(2):
                    heads = slice(i * HEADS, (i + 1) * HEADS)
                    scores[heads, at : at + 256] = jnp.where(
                        here < limits[i][:, rows], block[heads] * score_scale, -1e30
                    )
    highest = jnp.full((2 * HEADS, 1), -1e30, f32)
    for c in range(16):
        highest = jnp.maximum(
            highest, jnp.max(scores[:, c * 256 : (c + 1) * 256], axis=1, keepdims=True)
        )
    norm = jnp.zeros((2 * HEADS, 1), f32)
    for c in range(16):
        cols = slice(c * 256, (c + 1) * 256)
        weight = jnp.exp(scores[:, cols] - highest)
        scores[:, cols] = weight
        norm = norm + jnp.sum(weight, axis=1, keepdims=True)
    share = 1.0 / norm
    for c, (ref, rows, lanes) in enumerate(sets):
        probs = (scores[:, c * 256 : (c + 1) * 256] * share).astype(bf16)
        term = jnp.dot(probs, ref[rows, lanes], preferred_element_type=f32)
        for k in range(4):
            if c == 0:
                total[k] = term[:, k * 128 : (k + 1) * 128]
            else:
                total[k] += term[:, k * 128 : (k + 1) * 128]
    for h in range(HEADS):
        for k in range(4):
            at = h * DL + k * 128
            out_ref[:, at : at + 128] = total[k, pl.ds(h, 2, stride=HEADS), :].astype(bf16)


def attend(query, ids, near, far):
    return pl.pallas_call(
        attend_kernel,
        out_shape=jax.ShapeDtypeStruct((2, HEADS * DL), bf16),
        in_specs=[whole()] * 4,
        out_specs=whole(),
        scratch_shapes=[
            pltpu.VMEM((2 * HEADS, 4096), f32),
            pltpu.VMEM((4, 2 * HEADS, 128), f32),
        ],
        compiler_params=params(),
        cost_estimate=pl.CostEstimate(
            flops=2 * 256 * 4096 * 1152, bytes_accessed=6_000_000, transcendentals=256 * 4096
        ),
        name="attend",
    )(query, ids, near, far)


def level_from(value, away):
    pairs = [
        ((level + away) % LEVELS * 2 + core, level * 2 + core)
        for level in range(LEVELS)
        for core in range(2)
    ]
    return lax.ppermute(value, "ctx", pairs)


def swap(value):
    return lax.ppermute(value, "ctx", [(at, at ^ 1) for at in range(2 * LEVELS)])


def exchange(rows):
    parts = rows.reshape(PLANE, rows.shape[0] // PLANE, rows.shape[1])
    got = lax.all_to_all(parts, "pb", split_axis=0, concat_axis=0, tiled=True)
    return got.reshape(rows.shape)


def outer_levels(chunks):
    groups = [
        [(outer * 4 + inner) * 2 + core for outer in range(4)]
        for inner in range(4)
        for core in range(2)
    ]
    got = lax.all_to_all(
        chunks, "ctx", split_axis=0, concat_axis=0, axis_index_groups=groups, tiled=True
    )
    return got.reshape(chunks.shape[0] * chunks.shape[1], chunks.shape[2])


def local(q_latent, kv_cache, index_queries, index_weights, index_keys, q_blocks):
    z, y = pack(kv_cache.T, index_keys, index_queries, index_weights, q_blocks)
    held = outer_levels(z)
    y = lax.all_to_all(y, "pb", split_axis=0, concat_axis=0, tiled=True)
    across = swap(held)
    near = exchange(gather("near", NEAR, [held, across], y))
    others = [level_from(held, away) for away in (1, 15, 2)]
    swapped = [swap(other) for other in others]
    scores = score([held] + others + [across] + swapped, y)
    far = exchange(gather("far", FAR, others + swapped, y, scores))
    attention = attend(q_latent.reshape(2, HEADS, DQK), q_blocks, near, far)
    scores = far.reshape(PLANE, FAR[2], SENT_COLS)[:, :16, KV_COLS:]
    scores = scores.reshape(PLANE, 2, 32, 32).transpose(1, 2, 0, 3).reshape(2, 16384)
    return (attention, scores)


def solution(mesh):
    in_specs = (
        P(("ctx", "pb"), None),
        P("ctx", None),
        P(("ctx", "pb"), None),
        P(("ctx", "pb"), None),
        P(("ctx", "pb"), None),
        P(("ctx", "pb"), None),
    )
    out_specs = (P(("ctx", "pb"), None), P(("ctx", "pb"), None))
    return jax.shard_map(local, mesh=mesh, in_specs=in_specs, out_specs=out_specs, check_vma=False)
```

```python
import jax
import jax.numpy as jnp
from jax import lax
from jax.experimental import pallas as pl
from jax.experimental.pallas import tpu as pltpu
from jax.sharding import PartitionSpec as P

DL = 512
DQK = 576
ROT = DQK - DL
BLK = 64
IH = 64
ID = 128
HEADS = 128
PLANE = 16
LEVELS = 16
PIECE = BLK // PLANE
KV_COLS = PIECE * DQK
WIDTH = KV_COLS // 2
IDS_AT = KV_COLS + 4 * ID
Z_COLS = IDS_AT + 128
SENT_COLS = WIDTH + 128
AWAYS = (0, 1, 2, 14, 15)
VMEM_LIMIT = 24 * 1024 * 1024

score_scale = 192.0 ** (-0.5)
index_scale = 128.0 ** (-0.5)
f32 = jnp.float32
bf16 = jnp.bfloat16

NEAR = (0, 64, 12)
FAR = (64, 192, 32)


def params():
    return pltpu.CompilerParams(vmem_limit_bytes=VMEM_LIMIT)


def whole():
    return pl.BlockSpec(memory_space=pltpu.VMEM)


def anywhere():
    return pl.BlockSpec(memory_space=pl.ANY)


def iota(shape, dim):
    return lax.broadcasted_iota(jnp.int32, shape, dim)


def table_row(block):
    at = lax.axis_index("ctx")
    half = (block // 8 + at) % 2
    turn = (block // 16 - at // 2 + LEVELS) % 4
    order = jnp.where(turn == 3, 2, jnp.where(turn == 2, 3, turn))
    inner = block // 64 * 8 + block % 8
    return jnp.where(
        order == 0, half * 32 + inner, 64 + half * 96 + (order - 1) * 32 + inner
    )


def slot_shard(span, t):
    level = lax.axis_index("ctx") // 2
    if span is NEAR:
        away = (t % 32 // 8 * 4 + level % 4 - level + LEVELS) % LEVELS
        return jnp.where(away == 0, -1, t // 32 * 3 + away // 4 - 1)
    order = t % 96 // 32
    step = jnp.where(order == 0, 1, jnp.where(order == 1, 3, 2))
    away = (t % 32 // 8 * 4 + (level + step) % 4 - level + LEVELS) % LEVELS
    which = jnp.where(order == 1, away // 4, away // 4 - 1)
    return jnp.where((away > 2) & (away < 14), t // 96 * 8 + order * 3 + which, -1)


def pack_kernel(kv_ref, ik_ref, iq_ref, iw_ref, qb_ref, z_ref, y_ref, keys, rows):
    piece = lax.axis_index("pb")
    shard_keys = kv_ref.shape[1]
    line = iota((PIECE * 8, shard_keys), 0)
    source = (line % 8) * BLK + piece * PIECE + line // 8
    select = jnp.where(source == iota(source.shape, 1), 1.0, 0.0).astype(bf16)
    part = lax.dot_general(
        select, kv_ref[...], (((1,), (1,)), ((), ())), preferred_element_type=f32
    )
    keys[...] = ik_ref[...].astype(f32)
    ids = qb_ref[...].astype(f32)
    ids = jnp.concatenate([ids[0:1], ids[1:2], jnp.zeros((1, 64), f32)], axis=1)
    columns = []
    for r in range(0, PIECE, 2):
        pair = (part[r * 8 : (r + 1) * 8], part[(r + 1) * 8 : (r + 2) * 8])
        columns += [rows_of[:, :DL] for rows_of in pair] + [rows_of[:, DL:] for rows_of in pair]
    columns += [keys[pl.ds(j, 8, stride=4), :] for j in range(4)]
    columns.append(jnp.where(iota((8, 128), 0) == 0, ids, 0.0))
    chunk = jnp.concatenate(columns, axis=1).astype(bf16)
    for n in range(4):
        z_ref[n] = chunk
    for h in range(IH):
        rows[pl.ds(h, 2, stride=IH), :] = iq_ref[:, h * ID : (h + 1) * ID].astype(f32)
    weights = iw_ref[...].astype(f32)
    weights = jnp.concatenate([weights[0:1], weights[1:2]], axis=1)
    at = iota((16, 128), 0)
    tail = jnp.where(at == 0, weights, jnp.where(at == 1, ids, 0.0)).astype(bf16)
    head = rows[...].astype(bf16)
    for p in range(PLANE):
        y_ref[p, 0 : 2 * IH, :] = head
        y_ref[p, 2 * IH : 2 * IH + 16, :] = tail


def pack(kv_turned, index_keys, index_queries, index_weights, q_blocks):
    return pl.pallas_call(
        pack_kernel,
        out_shape=(
            jax.ShapeDtypeStruct((4, 8, Z_COLS), bf16),
            jax.ShapeDtypeStruct((PLANE, 2 * IH + 16, ID), bf16),
        ),
        in_specs=[whole()] * 5,
        out_specs=(whole(), whole()),
        scratch_shapes=[pltpu.VMEM((32, ID), f32), pltpu.VMEM((2 * IH, ID), f32)],
        compiler_params=params(),
        name="pack",
    )(kv_turned, index_keys, index_queries, index_weights, q_blocks)


def named_columns(span, ids):
    first, count, unused = span
    lane = iota((count, 128), 1)
    named = jnp.zeros((count, 128), f32)
    for n, row in enumerate(ids):
        place = table_row(row) - first
        hit = jnp.where(place == iota((count, row.shape[1]), 0), 1.0, 0.0)
        named = jnp.where(lane == n, jnp.max(hit, axis=1, keepdims=True), named)
    return named


def slot_codes(span, named):
    count = span[1]
    t, u = iota((count, count), 0), iota((count, count), 1)
    before = jnp.where((t // 8 == u // 8) & (u < t), 1.0, 0.0).astype(bf16)
    rank = jnp.dot(before, named.astype(bf16), preferred_element_type=f32)
    return jnp.where(named > 0.5, rank, -1.0)


def slot_keys(span, named):
    code = slot_codes(span, named)
    shard = slot_shard(span, iota((span[1], 1), 0)).astype(f32)
    return jnp.where((code >= 0.0) & (shard >= 0.0), shard * 2.0 + code, -1.0)


def gather_kernel(span, tables, y_ref, scores_ref, out_ref, onehot):
    first, count, slots = span
    rows = [
        y_ref[p, 2 * IH : 2 * IH + 16, :].astype(f32)[1:2, :64].astype(jnp.int32)
        for p in range(PLANE)
    ]
    keys = slot_keys(span, named_columns(span, rows))
    each = 2 * slots
    pad = -count % 128
    if pad:
        keys = jnp.concatenate([keys, jnp.zeros((pad, 128), f32)], axis=0)
    keys = keys.T[:PLANE, :count]
    keys = jnp.concatenate([keys, keys], axis=1)
    line, lane = iota((each, 2 * count), 0), iota((each, 2 * count), 1)
    half = jnp.where(line >= slots, 1, 0)
    wanted = jnp.where(
        half == jnp.where(lane >= count, 1, 0), line - half * slots, -5
    ).astype(f32)
    picks = [jnp.where(keys[p : p + 1] == wanted, 1.0, 0.0) for p in range(PLANE)]
    onehot[...] = jnp.concatenate(picks, axis=0).astype(bf16)
    for c in range(WIDTH // 384):
        rows = [
            ref[:, h * WIDTH + c * 384 : h * WIDTH + (c + 1) * 384]
            for h in range(2)
            for ref in tables
        ]
        out_ref[:, c * 384 : (c + 1) * 384] = jnp.dot(
            onehot[...], jnp.concatenate(rows, axis=0), preferred_element_type=f32
        ).astype(bf16)
    if scores_ref is not None:
        for p in range(PLANE):
            at = p * each
            out_ref[at : at + 16, WIDTH:] = scores_ref[p]
            out_ref[at + 16 : at + each, WIDTH:] = jnp.zeros((each - 16, 128), bf16)


def gather(name, span, tables, y, afters, scores=None):
    first, count, slots = span

    def body(*refs):
        refs = list(refs)
        held = [refs.pop(0) for table in tables]
        y_ref = refs.pop(0)
        scores_ref = None
        for after in afters:
            refs.pop(0)
        if scores is not None:
            scores_ref = refs.pop(0)
        gather_kernel(span, held, y_ref, scores_ref, *refs)

    operands = [*tables, y, *afters]
    in_specs = [whole()] * (len(tables) + 1) + [anywhere()] * len(afters)
    columns = WIDTH
    if scores is not None:
        operands.append(scores)
        in_specs.append(whole())
        columns = SENT_COLS
    return pl.pallas_call(
        body,
        out_shape=jax.ShapeDtypeStruct((PLANE * 2 * slots, columns), bf16),
        in_specs=in_specs,
        out_specs=whole(),
        scratch_shapes=[pltpu.VMEM((PLANE * 2 * slots, 2 * count), bf16)],
        compiler_params=params(),
        cost_estimate=pl.CostEstimate(
            flops=2 * PLANE * slots * 4 * count * WIDTH,
            bytes_accessed=3_000_000,
            transcendentals=0,
        ),
        name=name,
    )(*operands)


def serve_kernel(kv_ref, *refs):
    tables, outs = refs[:8], refs[9:]
    at = lax.axis_index("ctx")
    level = at // 2
    lines = []
    line = iota((32, 128), 0)
    for away in AWAYS:
        outer = (level + away) % LEVELS // 4
        for other in range(2):
            ref = tables[(0, 1, 3, 2)[away % 4] + 4 * other]
            values = jnp.where(line == outer * 8, ref[:, IDS_AT:].astype(f32), 0.0)
            lines.append(jnp.sum(values, axis=0, keepdims=True))
    lines += [jnp.full((6, 128), -1.0, f32)]
    ids = jnp.concatenate(lines, axis=0)[:, :64]
    own = (at * 8).astype(f32)
    lane = iota((16, 512), 1)
    codes = jnp.full((16, 512), -1.0, f32)
    taken = jnp.zeros((16, 1), f32)
    for b in range(8):
        hit = jnp.max(jnp.where(ids == own + b, 1.0, 0.0), axis=1, keepdims=True)
        codes = jnp.where((lane // BLK == b) & (hit > 0.5), taken, codes)
        taken = taken + hit
    row, lane = iota((128, 512), 0), iota((128, 512), 1)
    same = row % BLK == lane % BLK
    kind = (row // BLK).astype(f32)
    for n in range(len(AWAYS)):
        select = jnp.concatenate(
            [
                jnp.where(same & (codes[m : m + 1, :] == kind), 1.0, 0.0).astype(bf16)
                for m in (2 * n, 2 * n + 1)
            ],
            axis=0,
        )
        outs[n][...] = lax.dot_general(
            select, kv_ref[...], (((1,), (1,)), ((), ())), preferred_element_type=f32
        ).astype(bf16)


def serve(kv_turned, tables, after):
    return pl.pallas_call(
        serve_kernel,
        out_shape=tuple(jax.ShapeDtypeStruct((4 * BLK, DQK), bf16) for away in AWAYS),
        in_specs=[whole()] * 9 + [anywhere()],
        out_specs=(whole(),) * len(AWAYS),
        compiler_params=params(),
        cost_estimate=pl.CostEstimate(
            flops=2 * 10 * 128 * 512 * DQK, bytes_accessed=4_000_000, transcendentals=0
        ),
        name="serve",
    )(kv_turned, *tables, after)


def score_kernel(*refs):
    tables, y_ref, out_ref, keys = refs[:8], refs[8], refs[9], refs[10]
    tail = jnp.concatenate(
        [y_ref[p, 2 * IH : 2 * IH + 16, :].astype(f32)[0:1] for p in range(PLANE)], axis=0
    )
    weights = jnp.concatenate(
        [tail * index_scale, jnp.zeros((128 - PLANE, 128), f32)], axis=0
    ).T
    lane = iota((128, 128), 1)
    at = lax.axis_index("ctx")
    for n, ref in enumerate(tables):
        step = (0, 1, 3, 2)[n % 4]
        inner = (at // 2 + step) % 4
        core = (at + n // 4) % 2
        for outer in range(4):
            shard = (outer * 4 + inner) * 2 + core
            for j in range(4):
                cols = slice(KV_COLS + j * ID, KV_COLS + (j + 1) * ID)
                keys[pl.ds(shard * 32 + j, 8, stride=4), :] = ref[
                    outer * 8 : (outer + 1) * 8, cols
                ].astype(f32)
    key_rows = keys[...].astype(bf16)

    def peer(p, carry):
        products = lax.dot_general(
            y_ref[p, 0 : 2 * IH, :],
            key_rows,
            (((1,), (1,)), ((), ())),
            preferred_element_type=f32,
        )
        weight = jnp.sum(jnp.where(lane == p, weights, 0.0), axis=1, keepdims=True)
        active = jnp.maximum(products, 0.0) * weight
        lines = []
        for i in range(2):
            total = jnp.sum(active[i * IH : (i + 1) * IH], axis=0, keepdims=True)
            lines += [total[:, c * 128 : (c + 1) * 128] for c in range(8)]
        out_ref[p] = jnp.concatenate(lines, axis=0).astype(bf16)
        return carry

    lax.fori_loop(0, PLANE, peer, 0)


def score(tables, y):
    return pl.pallas_call(
        score_kernel,
        out_shape=jax.ShapeDtypeStruct((PLANE, 16, 128), bf16),
        in_specs=[whole()] * 9,
        out_specs=whole(),
        scratch_shapes=[pltpu.VMEM((1024, ID), f32)],
        compiler_params=params(),
        cost_estimate=pl.CostEstimate(
            flops=2 * 2048 * 128 * 1024, bytes_accessed=2_000_000, transcendentals=0
        ),
        name="score",
    )(*tables, y)


def attend_kernel(q_ref, ids_ref, near_ref, far_ref, *refs):
    count = len(AWAYS)
    mine, crossed = refs[:count], refs[count]
    out_ref, index_ref, scores, total, turned = refs[count + 1 :]
    direct = []
    for n in range(count):
        direct.append((mine[n], slice(0, 128)))
        direct.append((crossed, slice(n * 128, (n + 1) * 128)))
    at = lax.axis_index("ctx")
    rank = at * PLANE + lax.axis_index("pb")
    ids = ids_ref[...]
    own_block = 240 + rank * 2 // BLK
    own_row = table_row(own_block)
    offsets = [((rank * 2 + i) % BLK).astype(f32) for i in range(2)]
    query = jnp.concatenate([q_ref[0], q_ref[1]], axis=0)
    latent = query[:, :DL]
    rotary = query[:, DL:]
    nothing = jnp.zeros_like(rotary)
    padded = (
        jnp.concatenate([rotary, nothing], axis=1),
        jnp.concatenate([nothing, rotary], axis=1),
    )
    contract = (((1,), (1,)), ((), ()))
    sets = []
    filled = [0]
    tops = [jnp.full((HEADS, 128), -1e30, f32) for i in range(2)]

    def keep(block, place, limits, values):
        at, width = filled[0], block.shape[1]
        for i in range(2):
            heads = slice(i * HEADS, (i + 1) * HEADS)
            value = jnp.where(place < limits[i], block[heads] * score_scale, -1e30)
            scores[heads, at : at + width] = value
            for k in range(0, width, 128):
                tops[i] = jnp.maximum(tops[i], value[:, k : k + 128])
        sets.append((at, width, values))
        filled[0] += width

    def product(left, right):
        return lax.dot_general(left, right, contract, preferred_element_type=f32)

    count = 8 * len(direct)
    line = iota((count, 128), 0)
    lane = iota((count, 128), 1)
    named = jnp.zeros((count, 128), f32)
    shard = ids // 8
    away = (shard // 2 - at // 2 + LEVELS) % LEVELS
    turn = jnp.where(away < 3, away, jnp.where(away > 13, away - 11, -8))
    place = (turn * 2 + (shard + at) % 2) * 8 + ids % 8
    own_away = (own_block // 16 - at // 2 + LEVELS) % LEVELS
    own_turn = jnp.where(own_away < 3, own_away, jnp.where(own_away > 13, own_away - 11, -8))
    own_place = (own_turn * 2 + (own_block // 8 + at) % 2) * 8 + own_block % 8
    for i in range(2):
        hit = jnp.where(place[i : i + 1] == iota((count, ids.shape[1]), 0), 1.0, 0.0)
        named = jnp.where(lane == i, jnp.max(hit, axis=1, keepdims=True), named)
    members = named
    named = jnp.maximum(named[:, 0:1], named[:, 1:2])
    code = slot_codes((0, count, 2), jnp.broadcast_to(named, (count, 128)))
    chosen = code == (lane // BLK).astype(f32)
    limits = []
    for i in range(2):
        limit = jnp.where(line[:, 0:1] == own_place, offsets[i], 63.0) + 1.0
        limit = jnp.where(members[:, i : i + 1] > 0.5, limit, 0.0)
        limits.append(jnp.where(chosen, limit, 0.0))
    here = (iota((1, 128), 1) % BLK).astype(f32)
    here = jnp.concatenate([here, here], axis=1)
    for n in range(0, len(direct), 2):
        pair = direct[n : n + 2]
        block = product(
            latent, jnp.concatenate([ref[rows, :DL] for ref, rows in pair], axis=0)
        ) + product(
            rotary, jnp.concatenate([ref[rows, DL:] for ref, rows in pair], axis=0)
        )
        shown = [
            jnp.concatenate(
                [
                    jnp.sum(limit[m * 8 : (m + 1) * 8], axis=0, keepdims=True)
                    for m in (n, n + 1)
                ],
                axis=1,
            )
            for limit in limits
        ]
        keep(block, here, shown, [(ref, rows, slice(0, DL)) for ref, rows in pair])

    for span, ref, step in ((NEAR, near_ref, 384), (FAR, far_ref, 256)):
        first, count, slots = span
        one, two = named_columns(span, [ids[0:1]]), named_columns(span, [ids[1:2]])
        members = (one[:, 0:1], two[:, 0:1])
        keys = slot_keys(span, jnp.maximum(one, two))[:, 0:1]
        width = PLANE * 2 * slots
        line = iota((count, 128), 0)
        chosen = keys == (iota((1, width), 1) % slots).astype(f32)
        limits = []
        for i in range(2):
            limit = jnp.where(line[:, 0:1] + first == own_row, offsets[i], 63.0) + 1.0
            limit = jnp.where(members[i] > 0.5, limit, 0.0)
            limits.append(jnp.sum(jnp.where(chosen, limit, 0.0), axis=0, keepdims=True))
        lane = iota((1, width), 1)
        place = lane // (2 * slots) * PIECE + lane // slots % 2 * 2
        for k in range(width // step):
            rows = slice(k * step, (k + 1) * step)
            for parity in range(2):
                columns = slice(parity * DL, (parity + 1) * DL)
                block = product(latent, ref[rows, columns]) + product(
                    padded[parity], ref[rows, 2 * DL : 2 * DL + 128]
                )
                keep(
                    block,
                    (place[:, rows] + parity).astype(f32),
                    [limit[:, rows] for limit in limits],
                    [(ref, rows, columns)],
                )

    highest = jnp.max(jnp.concatenate(tops, axis=0), axis=1, keepdims=True)
    norm = jnp.zeros((2 * HEADS, 128), f32)
    for c in range(32):
        cols = slice(c * 128, (c + 1) * 128)
        weight = jnp.exp(scores[:, cols] - highest)
        scores[:, cols] = weight
        norm = norm + weight
    norm = jnp.sum(norm, axis=1, keepdims=True)
    share = 1.0 / norm
    for c, (at, width, values) in enumerate(sets):
        probs = (scores[:, at : at + width] * share).astype(bf16)
        rows = [ref[rows, columns] for ref, rows, columns in values]
        rows = rows[0] if len(rows) == 1 else jnp.concatenate(rows, axis=0)
        term = jnp.dot(probs, rows, preferred_element_type=f32)
        for k in range(4):
            if c == 0:
                total[k] = term[:, k * 128 : (k + 1) * 128]
            else:
                total[k] += term[:, k * 128 : (k + 1) * 128]
    for h in range(HEADS):
        for k in range(4):
            at = h * DL + k * 128
            out_ref[:, at : at + 128] = total[k, pl.ds(h, 2, stride=HEADS), :].astype(bf16)

    tiles = [
        far_ref[p * 2 * FAR[2] : p * 2 * FAR[2] + 16, WIDTH:].astype(f32)
        for p in range(PLANE)
    ]
    group = iota((16, 128), 1) // 32
    for c in range(4):
        for m in range(4):
            mixed = tiles[4 * m]
            for k in range(4):
                tile = tiles[4 * m + k]
                if k != c:
                    tile = pltpu.roll(tile, (k - c) * 32 % 128, 1)
                mixed = tile if k == 0 else jnp.where(group == k, tile, mixed)
            turned[(c * 4 + m) * 16 : (c * 4 + m + 1) * 16, :] = mixed
            for t in range(8):
                at = (t * 4 + c) * 512 + m * 128
                index_ref[:, at : at + 128] = turned[
                    pl.ds((c * 4 + m) * 16 + t, 2, stride=8), :
                ].astype(bf16)


def attend(query, ids, near, far, mine, crossed):
    return pl.pallas_call(
        attend_kernel,
        out_shape=(
            jax.ShapeDtypeStruct((2, HEADS * DL), bf16),
            jax.ShapeDtypeStruct((2, 16384), bf16),
        ),
        in_specs=[whole()] * (5 + len(mine)),
        out_specs=(whole(), whole()),
        scratch_shapes=[
            pltpu.VMEM((2 * HEADS, 4096), f32),
            pltpu.VMEM((4, 2 * HEADS, 128), f32),
            pltpu.VMEM((256, 128), f32),
        ],
        compiler_params=params(),
        cost_estimate=pl.CostEstimate(
            flops=2 * 256 * 4096 * 1152, bytes_accessed=6_000_000, transcendentals=256 * 4096
        ),
        name="attend",
    )(query, ids, near, far, *mine, crossed)


def join_kernel(*refs):
    out_ref = refs[-1]
    for n, ref in enumerate(refs[:-1]):
        out_ref[n * 128 : (n + 1) * 128, :] = ref[128:, :]


def join(parts):
    return pl.pallas_call(
        join_kernel,
        out_shape=jax.ShapeDtypeStruct((len(parts) * 128, DQK), bf16),
        in_specs=[whole()] * len(parts),
        out_specs=whole(),
        compiler_params=params(),
        cost_estimate=pl.CostEstimate(flops=0, bytes_accessed=2_000_000, transcendentals=0),
        name="join",
    )(*parts)


def level_from(value, away):
    pairs = [
        ((level + away) % LEVELS * 2 + core, level * 2 + core)
        for level in range(LEVELS)
        for core in range(2)
    ]
    return lax.ppermute(value, "ctx", pairs)


def swap(value):
    return lax.ppermute(value, "ctx", [(at, at ^ 1) for at in range(2 * LEVELS)])


def exchange(rows):
    parts = rows.reshape(PLANE, rows.shape[0] // PLANE, rows.shape[1])
    got = lax.all_to_all(parts, "pb", split_axis=0, concat_axis=0, tiled=True)
    return got.reshape(rows.shape)


def outer_levels(chunks):
    groups = [
        [(outer * 4 + inner) * 2 + core for outer in range(4)]
        for inner in range(4)
        for core in range(2)
    ]
    got = lax.all_to_all(
        chunks, "ctx", split_axis=0, concat_axis=0, axis_index_groups=groups, tiled=True
    )
    return got.reshape(chunks.shape[0] * chunks.shape[1], chunks.shape[2])


def local(q_latent, kv_cache, index_queries, index_weights, index_keys, q_blocks):
    kv_turned = kv_cache.T
    z, y = pack(kv_turned, index_keys, index_queries, index_weights, q_blocks)
    held = outer_levels(z)
    y = lax.all_to_all(y, "pb", split_axis=0, concat_axis=0, tiled=True)
    across = swap(held)
    others = [level_from(held, away) for away in (1, 15, 2)]
    near = exchange(gather("near", NEAR, [held, across], y, others))
    swapped = [swap(other) for other in others]
    tables = [held] + others + [across] + swapped
    scores = score(tables, y)
    sent = gather("far", FAR, others + swapped, y, [near], scores)
    served = serve(kv_turned, tables, sent)
    far = exchange(sent)
    mine = [served[0]]
    for away in AWAYS[1:]:
        mine.append(level_from(served[AWAYS.index(-away % LEVELS)], away))
    crossed = swap(join(mine))
    query = q_latent.reshape(2, HEADS, DQK)
    return tuple(attend(query, q_blocks, near, far, mine, crossed))


def solution(mesh):
    in_specs = (
        P(("ctx", "pb"), None),
        P("ctx", None),
        P(("ctx", "pb"), None),
        P(("ctx", "pb"), None),
        P(("ctx", "pb"), None),
        P(("ctx", "pb"), None),
    )
    out_specs = (P(("ctx", "pb"), None), P(("ctx", "pb"), None))
    return jax.shard_map(local, mesh=mesh, in_specs=in_specs, out_specs=out_specs, check_vma=False)
```

```python
import jax
import jax.numpy as jnp
from jax import lax
from jax.experimental import pallas as pl
from jax.experimental.pallas import tpu as pltpu
from jax.sharding import PartitionSpec as P

DL = 512
DQK = 576
ROT = DQK - DL
BLK = 64
IH = 64
ID = 128
HEADS = 128
PLANE = 16
LEVELS = 16
PIECE = BLK // PLANE
KV_COLS = PIECE * DQK
WIDTH = KV_COLS // 2
IDS_AT = KV_COLS + 4 * ID
Z_COLS = IDS_AT + 128
SENT_COLS = KV_COLS + 128
AWAYS = (0, 1, 2, 14, 15)
VMEM_LIMIT = 24 * 1024 * 1024

score_scale = 192.0 ** (-0.5)
index_scale = 128.0 ** (-0.5)
f32 = jnp.float32
bf16 = jnp.bfloat16

NEAR = (0, 64, 12)
FAR = (64, 192, 32)


def params():
    return pltpu.CompilerParams(vmem_limit_bytes=VMEM_LIMIT)


def whole():
    return pl.BlockSpec(memory_space=pltpu.VMEM)


def anywhere():
    return pl.BlockSpec(memory_space=pl.ANY)


def iota(shape, dim):
    return lax.broadcasted_iota(jnp.int32, shape, dim)


def table_row(block):
    at = lax.axis_index("ctx")
    half = (block // 8 + at) % 2
    turn = (block // 16 - at // 2 + LEVELS) % 4
    order = jnp.where(turn == 3, 2, jnp.where(turn == 2, 3, turn))
    inner = block // 64 * 8 + block % 8
    return jnp.where(
        order == 0, half * 32 + inner, 64 + half * 96 + (order - 1) * 32 + inner
    )


def slot_shard(span, t):
    level = lax.axis_index("ctx") // 2
    if span is NEAR:
        away = (t % 32 // 8 * 4 + level % 4 - level + LEVELS) % LEVELS
        return jnp.where(away == 0, -1, t // 32 * 3 + away // 4 - 1)
    order = t % 96 // 32
    step = jnp.where(order == 0, 1, jnp.where(order == 1, 3, 2))
    away = (t % 32 // 8 * 4 + (level + step) % 4 - level + LEVELS) % LEVELS
    which = jnp.where(order == 1, away // 4, away // 4 - 1)
    return jnp.where((away > 2) & (away < 14), t // 96 * 8 + order * 3 + which, -1)


def pack_kernel(*refs):
    sources, (z_ref, y_ref, keys, rows), targets, sem = refs[:5], refs[5:9], refs[9:14], refs[14]
    copies = [
        pltpu.make_async_copy(source, target, sem.at[n])
        for n, (source, target) in enumerate(zip(sources, targets))
    ]
    for copy in copies:
        copy.start()
    for copy in copies:
        copy.wait()
    kv_ref, ik_ref, iq_ref, iw_ref, qb_ref = targets
    piece = lax.axis_index("pb")
    shard_keys = kv_ref.shape[1]
    line = iota((PIECE * 8, shard_keys), 0)
    source = (line % 8) * BLK + piece * PIECE + line // 8
    select = jnp.where(source == iota(source.shape, 1), 1.0, 0.0).astype(bf16)
    part = lax.dot_general(
        select, kv_ref[...], (((1,), (1,)), ((), ())), preferred_element_type=f32
    )
    keys[...] = ik_ref[...].astype(f32)
    ids = qb_ref[...].astype(f32)
    ids = jnp.concatenate([ids[0:1], ids[1:2], jnp.zeros((1, 64), f32)], axis=1)
    columns = []
    for r in range(0, PIECE, 2):
        pair = (part[r * 8 : (r + 1) * 8], part[(r + 1) * 8 : (r + 2) * 8])
        columns += [rows_of[:, :DL] for rows_of in pair] + [rows_of[:, DL:] for rows_of in pair]
    columns += [keys[pl.ds(j, 8, stride=4), :] for j in range(4)]
    columns.append(jnp.where(iota((8, 128), 0) == 0, ids, 0.0))
    chunk = jnp.concatenate(columns, axis=1).astype(bf16)
    for n in range(4):
        z_ref[n] = chunk
    for h in range(IH):
        rows[pl.ds(h, 2, stride=IH), :] = iq_ref[:, h * ID : (h + 1) * ID].astype(f32)
    weights = iw_ref[...].astype(f32)
    weights = jnp.concatenate([weights[0:1], weights[1:2]], axis=1)
    at = iota((16, 128), 0)
    tail = jnp.where(at == 0, weights, jnp.where(at == 1, ids, 0.0)).astype(bf16)
    head = rows[...].astype(bf16)
    for p in range(PLANE):
        y_ref[p, 0 : 2 * IH, :] = head
        y_ref[p, 2 * IH : 2 * IH + 16, :] = tail


def pack(kv_turned, index_keys, index_queries, index_weights, q_blocks):
    return pl.pallas_call(
        pack_kernel,
        out_shape=(
            jax.ShapeDtypeStruct((4, 8, Z_COLS), bf16),
            jax.ShapeDtypeStruct((PLANE, 2 * IH + 16, ID), bf16),
        ),
        in_specs=[anywhere()] * 5,
        out_specs=(whole(), whole()),
        scratch_shapes=[pltpu.VMEM((32, ID), f32), pltpu.VMEM((2 * IH, ID), f32)]
        + [
            pltpu.VMEM(value.shape, value.dtype)
            for value in (kv_turned, index_keys, index_queries, index_weights, q_blocks)
        ]
        + [pltpu.SemaphoreType.DMA((5,))],
        compiler_params=params(),
        name="pack",
    )(kv_turned, index_keys, index_queries, index_weights, q_blocks)


def named_columns(span, ids):
    first, count, unused = span
    lane = iota((count, 128), 1)
    named = jnp.zeros((count, 128), f32)
    for n, row in enumerate(ids):
        place = table_row(row) - first
        hit = jnp.where(place == iota((count, row.shape[1]), 0), 1.0, 0.0)
        named = jnp.where(lane == n, jnp.max(hit, axis=1, keepdims=True), named)
    return named


def slot_codes(span, named):
    count = span[1]
    t, u = iota((count, count), 0), iota((count, count), 1)
    before = jnp.where((t // 8 == u // 8) & (u < t), 1.0, 0.0).astype(bf16)
    rank = jnp.dot(before, named.astype(bf16), preferred_element_type=f32)
    return jnp.where(named > 0.5, rank, -1.0)


def slot_keys(span, named):
    code = slot_codes(span, named)
    shard = slot_shard(span, iota((span[1], 1), 0)).astype(f32)
    return jnp.where((code >= 0.0) & (shard >= 0.0), shard * 2.0 + code, -1.0)


def gather_kernel(span, tables, y_ref, scores_ref, out_ref, onehot):
    first, count, slots = span
    rows = [
        y_ref[p, 2 * IH : 2 * IH + 16, :].astype(f32)[1:2, :64].astype(jnp.int32)
        for p in range(PLANE)
    ]
    keys = slot_keys(span, named_columns(span, rows))
    halves = 2 if span is NEAR else 1
    each = halves * slots
    pad = -count % 128
    keys = jnp.concatenate([keys, jnp.zeros((pad, 128), f32)], axis=0)
    keys = jnp.concatenate([keys.T[:PLANE, :count]] * halves, axis=1)
    line, lane = iota((each, halves * count), 0), iota((each, halves * count), 1)
    half = jnp.where(line >= slots, 1, 0)
    there = jnp.where(lane >= count, 1, 0)
    wanted = jnp.where(half == there, line - half * slots, -5).astype(f32)
    picks = [jnp.where(keys[p : p + 1] == wanted, 1.0, 0.0) for p in range(PLANE)]
    onehot[...] = jnp.concatenate(picks, axis=0).astype(bf16)
    columns = KV_COLS // halves
    for c in range(columns // 384):
        rows = [
            ref[:, h * columns + c * 384 : h * columns + (c + 1) * 384]
            for h in range(halves)
            for ref in tables
        ]
        out_ref[:, c * 384 : (c + 1) * 384] = jnp.dot(
            onehot[...], jnp.concatenate(rows, axis=0), preferred_element_type=f32
        ).astype(bf16)
    if scores_ref is not None:
        for p in range(PLANE):
            at = p * each
            out_ref[at : at + 16, columns:] = scores_ref[p]
            out_ref[at + 16 : at + each, columns:] = jnp.zeros((each - 16, 128), bf16)


def gather(name, span, tables, y, afters, scores=None):
    first, count, slots = span

    def body(*refs):
        refs = list(refs)
        held = [refs.pop(0) for table in tables]
        y_ref = refs.pop(0)
        scores_ref = None
        for after in afters:
            refs.pop(0)
        if scores is not None:
            scores_ref = refs.pop(0)
        gather_kernel(span, held, y_ref, scores_ref, *refs)

    halves = 2 if span is NEAR else 1
    operands = [*tables, y, *afters]
    in_specs = [whole()] * (len(tables) + 1) + [anywhere()] * len(afters)
    columns = WIDTH
    if scores is not None:
        operands.append(scores)
        in_specs.append(whole())
        columns = SENT_COLS
    return pl.pallas_call(
        body,
        out_shape=jax.ShapeDtypeStruct((PLANE * halves * slots, columns), bf16),
        in_specs=in_specs,
        out_specs=whole(),
        scratch_shapes=[pltpu.VMEM((PLANE * halves * slots, halves * count), bf16)],
        compiler_params=params(),
        cost_estimate=pl.CostEstimate(
            flops=2 * PLANE * slots * 4 * count * WIDTH,
            bytes_accessed=3_000_000,
            transcendentals=0,
        ),
        name=name,
    )(*operands)


def serve_kernel(kv_ref, *refs):
    tables, outs = refs[:8], refs[9:]
    at = lax.axis_index("ctx")
    level = at // 2
    lines = []
    line = iota((32, 128), 0)
    for away in AWAYS:
        outer = (level + away) % LEVELS // 4
        for other in range(2):
            ref = tables[(0, 1, 3, 2)[away % 4] + 4 * other]
            values = jnp.where(line == outer * 8, ref[:, IDS_AT:].astype(f32), 0.0)
            lines.append(jnp.sum(values, axis=0, keepdims=True))
    lines += [jnp.full((6, 128), -1.0, f32)]
    ids = jnp.concatenate(lines, axis=0)[:, :64]
    own = (at * 8).astype(f32)
    lane = iota((16, 512), 1)
    codes = jnp.full((16, 512), -1.0, f32)
    taken = jnp.zeros((16, 1), f32)
    for b in range(8):
        hit = jnp.max(jnp.where(ids == own + b, 1.0, 0.0), axis=1, keepdims=True)
        codes = jnp.where((lane // BLK == b) & (hit > 0.5), taken, codes)
        taken = taken + hit
    row, lane = iota((64, 512), 0), iota((64, 512), 1)
    kind = (row // 32).astype(f32)
    for n in range(len(AWAYS)):
        select = jnp.concatenate(
            [
                jnp.where(
                    (row % 32 + 32 * half == lane % BLK) & (codes[m : m + 1, :] == kind),
                    1.0,
                    0.0,
                )
                for half in range(2)
                for m in (2 * n, 2 * n + 1)
            ],
            axis=0,
        ).astype(bf16)
        got = lax.dot_general(
            select, kv_ref[...], (((1,), (1,)), ((), ())), preferred_element_type=f32
        )
        got = (got[:128], got[128:])
        columns = [part[:, :DL] for part in got] + [part[:, DL:] for part in got]
        outs[n][...] = jnp.concatenate(columns, axis=1).astype(bf16)


def serve(kv_turned, tables, after):
    return pl.pallas_call(
        serve_kernel,
        out_shape=tuple(jax.ShapeDtypeStruct((2 * BLK, WIDTH), bf16) for away in AWAYS),
        in_specs=[whole()] * 9 + [anywhere()],
        out_specs=(whole(),) * len(AWAYS),
        compiler_params=params(),
        cost_estimate=pl.CostEstimate(
            flops=2 * 10 * 128 * 512 * DQK, bytes_accessed=4_000_000, transcendentals=0
        ),
        name="serve",
    )(kv_turned, *tables, after)


def score_kernel(*refs):
    tables, y_ref, out_ref, keys = refs[:8], refs[8], refs[9], refs[10]
    tail = jnp.concatenate(
        [y_ref[p, 2 * IH : 2 * IH + 16, :].astype(f32)[0:1] for p in range(PLANE)], axis=0
    )
    weights = jnp.concatenate(
        [tail * index_scale, jnp.zeros((128 - PLANE, 128), f32)], axis=0
    ).T
    lane = iota((128, 128), 1)
    at = lax.axis_index("ctx")
    for n, ref in enumerate(tables):
        step = (0, 1, 3, 2)[n % 4]
        inner = (at // 2 + step) % 4
        core = (at + n // 4) % 2
        for outer in range(4):
            shard = (outer * 4 + inner) * 2 + core
            for j in range(4):
                cols = slice(KV_COLS + j * ID, KV_COLS + (j + 1) * ID)
                keys[pl.ds(shard * 32 + j, 8, stride=4), :] = ref[
                    outer * 8 : (outer + 1) * 8, cols
                ].astype(f32)
    key_rows = keys[...].astype(bf16)

    def peers(g, carry):
        products = lax.dot_general(
            y_ref[pl.ds(g * 4, 4), 0 : 2 * IH, :].reshape(8 * IH, ID),
            key_rows,
            (((1,), (1,)), ((), ())),
            preferred_element_type=f32,
        )
        for m in range(4):
            weight = jnp.sum(
                jnp.where(lane == g * 4 + m, weights, 0.0), axis=1, keepdims=True
            )
            active = jnp.maximum(products[m * 2 * IH : (m + 1) * 2 * IH], 0.0) * weight
            lines = []
            for i in range(2):
                total = jnp.sum(active[i * IH : (i + 1) * IH], axis=0, keepdims=True)
                lines += [total[:, c * 128 : (c + 1) * 128] for c in range(8)]
            out_ref[g * 4 + m] = jnp.concatenate(lines, axis=0).astype(bf16)
        return carry

    lax.fori_loop(0, PLANE // 4, peers, 0)


def score(tables, y):
    return pl.pallas_call(
        score_kernel,
        out_shape=jax.ShapeDtypeStruct((PLANE, 16, 128), bf16),
        in_specs=[whole()] * 9,
        out_specs=whole(),
        scratch_shapes=[pltpu.VMEM((1024, ID), f32)],
        compiler_params=params(),
        cost_estimate=pl.CostEstimate(
            flops=2 * 2048 * 128 * 1024, bytes_accessed=2_000_000, transcendentals=0
        ),
        name="score",
    )(*tables, y)


def attend_kernel(q_ref, ids_ref, near_ref, far_ref, *refs):
    count = len(AWAYS)
    mine, crossed = refs[:count], refs[count]
    out_ref, index_ref, scores, total, turned, direct, sem = refs[count + 1 :]
    copies = []
    for n in range(count):
        for other in range(2):
            source = crossed.at[pl.ds(n * 64, 64)] if other else mine[n].at[pl.ds(0, 64)]
            target = direct.at[pl.ds((2 * n + other) * 64, 64)]
            copies.append(pltpu.make_async_copy(source, target, sem.at[2 * n + other]))
    for copy in copies:
        copy.start()
    ctx = lax.axis_index("ctx")
    rank = ctx * PLANE + lax.axis_index("pb")
    ids = ids_ref[...]
    own_block = 240 + rank * 2 // BLK
    own_row = table_row(own_block)
    offsets = [((rank * 2 + i) % BLK).astype(f32) for i in range(2)]
    query = jnp.concatenate([q_ref[0], q_ref[1]], axis=0)
    latent = query[:, :DL]
    rotary = query[:, DL:]
    nothing = jnp.zeros_like(rotary)
    padded = (
        jnp.concatenate([rotary, nothing], axis=1),
        jnp.concatenate([nothing, rotary], axis=1),
    )
    contract = (((1,), (1,)), ((), ()))
    sets = []
    filled = [0]
    tops = [jnp.full((HEADS, 128), -1e30, f32) for i in range(2)]

    def keep(block, place, limits, values):
        at, width = filled[0], block.shape[1]
        for i in range(2):
            heads = slice(i * HEADS, (i + 1) * HEADS)
            value = jnp.where(place < limits[i], block[heads] * score_scale, -1e30)
            scores[heads, at : at + width] = value
            for k in range(0, width, 128):
                tops[i] = jnp.maximum(tops[i], value[:, k : k + 128])
        sets.append((at, width, values))
        filled[0] += width

    def product(left, right):
        return lax.dot_general(left, right, contract, preferred_element_type=f32)

    for span, ref, step in ((NEAR, near_ref, 384), (FAR, far_ref, 256)):
        first, count, slots = span
        one, two = named_columns(span, [ids[0:1]]), named_columns(span, [ids[1:2]])
        members = (one[:, 0:1], two[:, 0:1])
        keys = slot_keys(span, jnp.maximum(one, two))[:, 0:1]
        halves = 2 if span is NEAR else 1
        width = PLANE * halves * slots
        line = iota((count, 128), 0)
        chosen = keys == (iota((1, width), 1) % slots).astype(f32)
        limits = []
        for i in range(2):
            limit = jnp.where(line[:, 0:1] + first == own_row, offsets[i], 63.0) + 1.0
            limit = jnp.where(members[i] > 0.5, limit, 0.0)
            limits.append(jnp.sum(jnp.where(chosen, limit, 0.0), axis=0, keepdims=True))
        lane = iota((1, width), 1)
        place = lane // (halves * slots) * PIECE
        if halves == 2:
            place = place + lane // slots % 2 * 2
        for k in range(width // step):
            rows = slice(k * step, (k + 1) * step)
            for r in range(PIECE // halves):
                half, parity = r // 2, r % 2
                at = half * WIDTH + parity * DL
                columns = slice(at, at + DL)
                turn = half * WIDTH + 2 * DL
                block = product(latent, ref[rows, columns]) + product(
                    padded[parity], ref[rows, turn : turn + 128]
                )
                keep(
                    block,
                    (place[:, rows] + r).astype(f32),
                    [limit[:, rows] for limit in limits],
                    [(ref, rows, columns)],
                )

    count = 16 * len(AWAYS)
    line = iota((count, 128), 0)
    lane = iota((count, 128), 1)
    named = jnp.zeros((count, 128), f32)
    shard = ids // 8
    away = (shard // 2 - ctx // 2 + LEVELS) % LEVELS
    turn = jnp.where(away < 3, away, jnp.where(away > 13, away - 11, -8))
    place = (turn * 2 + (shard + ctx) % 2) * 8 + ids % 8
    own_away = (own_block // 16 - ctx // 2 + LEVELS) % LEVELS
    own_turn = jnp.where(own_away < 3, own_away, jnp.where(own_away > 13, own_away - 11, -8))
    own_place = (own_turn * 2 + (own_block // 8 + ctx) % 2) * 8 + own_block % 8
    for i in range(2):
        hit = jnp.where(place[i : i + 1] == iota((count, ids.shape[1]), 0), 1.0, 0.0)
        named = jnp.where(lane == i, jnp.max(hit, axis=1, keepdims=True), named)
    members = named
    named = jnp.maximum(named[:, 0:1], named[:, 1:2])
    code = slot_codes((0, count, 2), jnp.broadcast_to(named, (count, 128)))
    chosen = code == (lane // 32 % 2).astype(f32)
    limits = []
    for i in range(2):
        limit = jnp.where(line[:, 0:1] == own_place, offsets[i], 63.0) + 1.0
        limit = jnp.where(members[:, i : i + 1] > 0.5, limit, 0.0)
        limits.append(jnp.where(chosen, limit, 0.0))
    low = iota((1, 128), 1) < 64
    shown = [
        [
            jnp.where(
                low,
                jnp.sum(limit[n * 8 : (n + 1) * 8], axis=0, keepdims=True),
                jnp.sum(limit[(n + 1) * 8 : (n + 2) * 8], axis=0, keepdims=True),
            )
            for n in range(0, 2 * len(AWAYS), 2)
        ]
        for limit in limits
    ]
    here = iota((1, 128), 1) % 32
    for copy in copies:
        copy.wait()
    for first, last in ((0, 2), (2, 4), (4, 5)):
        rows = slice(first * 128, last * 128)
        for parity in range(2):
            columns = slice(parity * DL, (parity + 1) * DL)
            block = product(latent, direct[rows, columns]) + product(
                padded[parity], direct[rows, 2 * DL : 2 * DL + 128]
            )
            keep(
                block,
                jnp.concatenate([(here + 32 * parity).astype(f32)] * (last - first), axis=1),
                [jnp.concatenate(each[first:last], axis=1) for each in shown],
                [(direct, rows, columns)],
            )

    highest = jnp.max(jnp.concatenate(tops, axis=0), axis=1, keepdims=True)
    norm = jnp.zeros((2 * HEADS, 128), f32)
    for c in range(32):
        cols = slice(c * 128, (c + 1) * 128)
        weight = jnp.exp(scores[:, cols] - highest)
        scores[:, cols] = weight
        norm = norm + weight
    norm = jnp.sum(norm, axis=1, keepdims=True)
    share = 1.0 / norm
    for c, (at, width, values) in enumerate(sets):
        probs = (scores[:, at : at + width] * share).astype(bf16)
        rows = [ref[rows, columns] for ref, rows, columns in values]
        rows = rows[0] if len(rows) == 1 else jnp.concatenate(rows, axis=0)
        term = jnp.dot(probs, rows, preferred_element_type=f32)
        for k in range(4):
            if c == 0:
                total[k] = term[:, k * 128 : (k + 1) * 128]
            else:
                total[k] += term[:, k * 128 : (k + 1) * 128]
    for h in range(HEADS):
        for k in range(4):
            at = h * DL + k * 128
            out_ref[:, at : at + 128] = total[k, pl.ds(h, 2, stride=HEADS), :].astype(bf16)

    tiles = [
        far_ref[p * FAR[2] : p * FAR[2] + 16, KV_COLS:].astype(f32)
        for p in range(PLANE)
    ]
    group = iota((16, 128), 1) // 32
    for c in range(4):
        for m in range(4):
            mixed = tiles[4 * m]
            for k in range(4):
                tile = tiles[4 * m + k]
                if k != c:
                    tile = pltpu.roll(tile, (k - c) * 32 % 128, 1)
                mixed = tile if k == 0 else jnp.where(group == k, tile, mixed)
            turned[(c * 4 + m) * 16 : (c * 4 + m + 1) * 16, :] = mixed
            for t in range(8):
                at = (t * 4 + c) * 512 + m * 128
                index_ref[:, at : at + 128] = turned[
                    pl.ds((c * 4 + m) * 16 + t, 2, stride=8), :
                ].astype(bf16)


def attend(query, ids, near, far, mine, crossed):
    return pl.pallas_call(
        attend_kernel,
        out_shape=(
            jax.ShapeDtypeStruct((2, HEADS * DL), bf16),
            jax.ShapeDtypeStruct((2, 16384), bf16),
        ),
        in_specs=[whole()] * 4 + [anywhere()] * (1 + len(mine)),
        out_specs=(whole(), whole()),
        scratch_shapes=[
            pltpu.VMEM((2 * HEADS, 4096), f32),
            pltpu.VMEM((4, 2 * HEADS, 128), f32),
            pltpu.VMEM((256, 128), f32),
            pltpu.VMEM((128 * len(AWAYS), WIDTH), bf16),
            pltpu.SemaphoreType.DMA((2 * len(AWAYS),)),
        ],
        compiler_params=params(),
        cost_estimate=pl.CostEstimate(
            flops=2 * 256 * 4096 * 1152, bytes_accessed=6_000_000, transcendentals=256 * 4096
        ),
        name="attend",
    )(query, ids, near, far, *mine, crossed)


def two_levels_on(value):
    pairs = [
        ((level + (2, -2)[core]) % LEVELS * 2 + core, level * 2 + core)
        for level in range(LEVELS)
        for core in range(2)
    ]
    return lax.ppermute(value, "ctx", pairs)


def join_kernel(*refs):
    out_ref = refs[-1]
    for n, ref in enumerate(refs[:-1]):
        out_ref[n * 64 : (n + 1) * 64, :] = ref[64:, :]


def join(parts):
    return pl.pallas_call(
        join_kernel,
        out_shape=jax.ShapeDtypeStruct((len(parts) * 64, WIDTH), bf16),
        in_specs=[whole()] * len(parts),
        out_specs=whole(),
        compiler_params=params(),
        cost_estimate=pl.CostEstimate(flops=0, bytes_accessed=2_000_000, transcendentals=0),
        name="join",
    )(*parts)


def level_from(value, away):
    pairs = [
        ((level + away) % LEVELS * 2 + core, level * 2 + core)
        for level in range(LEVELS)
        for core in range(2)
    ]
    return lax.ppermute(value, "ctx", pairs)


def swap(value):
    return lax.ppermute(value, "ctx", [(at, at ^ 1) for at in range(2 * LEVELS)])


def exchange(rows):
    parts = rows.reshape(PLANE, rows.shape[0] // PLANE, rows.shape[1])
    got = lax.all_to_all(parts, "pb", split_axis=0, concat_axis=0, tiled=True)
    return got.reshape(rows.shape)


def outer_levels(chunks):
    groups = [
        [(outer * 4 + inner) * 2 + core for outer in range(4)]
        for inner in range(4)
        for core in range(2)
    ]
    got = lax.all_to_all(
        chunks, "ctx", split_axis=0, concat_axis=0, axis_index_groups=groups, tiled=True
    )
    return got.reshape(chunks.shape[0] * chunks.shape[1], chunks.shape[2])


def local(q_latent, kv_cache, index_queries, index_weights, index_keys, q_blocks):
    kv_turned = kv_cache.T
    z, y = pack(kv_turned, index_keys, index_queries, index_weights, q_blocks)
    held = outer_levels(z)
    y = lax.all_to_all(y, "pb", split_axis=0, concat_axis=0, tiled=True)
    across = swap(held)
    others = [level_from(held, 1), level_from(held, 15), two_levels_on(held)]
    near = exchange(gather("near", NEAR, [held, across], y, others))
    swapped = [swap(other) for other in others]
    tables = [held] + others + [across] + swapped
    scores = score(tables, y)
    sent = gather("far", FAR, others + swapped, y, [near], scores)
    served = serve(kv_turned, tables, sent)
    far = exchange(sent)
    mine = [served[0]]
    for away in AWAYS[1:]:
        mine.append(level_from(served[AWAYS.index(-away % LEVELS)], away))
    crossed = swap(join(mine))
    query = q_latent.reshape(2, HEADS, DQK)
    return tuple(attend(query, q_blocks, near, far, mine, crossed))


def solution(mesh):
    in_specs = (
        P(("ctx", "pb"), None),
        P("ctx", None),
        P(("ctx", "pb"), None),
        P(("ctx", "pb"), None),
        P(("ctx", "pb"), None),
        P(("ctx", "pb"), None),
    )
    out_specs = (P(("ctx", "pb"), None), P(("ctx", "pb"), None))
    return jax.shard_map(local, mesh=mesh, in_specs=in_specs, out_specs=out_specs, check_vma=False)
```

```python
import jax
import jax.numpy as jnp
from jax import lax
from jax.experimental import pallas as pl
from jax.experimental.pallas import tpu as pltpu
from jax.sharding import PartitionSpec as P

DL = 512
DQK = 576
ROT = DQK - DL
BLK = 64
IH = 64
ID = 128
HEADS = 128
PLANE = 16
LEVELS = 16
PIECE = BLK // PLANE
KV_COLS = PIECE * DQK
WIDTH = KV_COLS // 2
IDS_AT = KV_COLS + 4 * ID
Z_COLS = IDS_AT + 128
SENT_COLS = KV_COLS + 128
AWAYS = (0, 1, 2, 14, 15)
VMEM_LIMIT = 24 * 1024 * 1024

score_scale = 192.0 ** (-0.5)
index_scale = 128.0 ** (-0.5)
f32 = jnp.float32
bf16 = jnp.bfloat16

NEAR = (0, 64, 12)
FAR = (64, 192, 32)


def params(limit=VMEM_LIMIT):
    return pltpu.CompilerParams(vmem_limit_bytes=limit)


def whole():
    return pl.BlockSpec(memory_space=pltpu.VMEM)


def anywhere():
    return pl.BlockSpec(memory_space=pl.ANY)


def main_memory():
    return pl.BlockSpec(memory_space=pltpu.HBM)


def iota(shape, dim):
    return lax.broadcasted_iota(jnp.int32, shape, dim)


def table_row(block):
    at = lax.axis_index("ctx")
    half = (block // 8 + at) % 2
    turn = (block // 16 - at // 2 + LEVELS) % 4
    order = jnp.where(turn == 3, 2, jnp.where(turn == 2, 3, turn))
    inner = block // 64 * 8 + block % 8
    return jnp.where(
        order == 0, half * 32 + inner, 64 + half * 96 + (order - 1) * 32 + inner
    )


def slot_shard(span, t):
    level = lax.axis_index("ctx") // 2
    if span is NEAR:
        away = (t % 32 // 8 * 4 + level % 4 - level + LEVELS) % LEVELS
        return jnp.where(away == 0, -1, t // 32 * 3 + away // 4 - 1)
    order = t % 96 // 32
    step = jnp.where(order == 0, 1, jnp.where(order == 1, 3, 2))
    away = (t % 32 // 8 * 4 + (level + step) % 4 - level + LEVELS) % LEVELS
    which = jnp.where(order == 1, away // 4, away // 4 - 1)
    return jnp.where((away > 2) & (away < 14), t // 96 * 8 + order * 3 + which, -1)


def pack_kernel(*refs):
    sources, (z_ref, y_ref, keys, rows), targets, sem = refs[:5], refs[5:9], refs[9:14], refs[14]
    copies = [
        pltpu.make_async_copy(source, target, sem.at[n])
        for n, (source, target) in enumerate(zip(sources, targets))
    ]
    for copy in copies:
        copy.start()
    for copy in copies:
        copy.wait()
    kv_ref, ik_ref, iq_ref, iw_ref, qb_ref = targets
    piece = lax.axis_index("pb")
    shard_keys = kv_ref.shape[1]
    line = iota((PIECE * 8, shard_keys), 0)
    source = (line % 8) * BLK + piece * PIECE + line // 8
    select = jnp.where(source == iota(source.shape, 1), 1.0, 0.0).astype(bf16)
    part = lax.dot_general(
        select, kv_ref[...], (((1,), (1,)), ((), ())), preferred_element_type=f32
    )
    keys[...] = ik_ref[...].astype(f32)
    ids = qb_ref[...].astype(f32)
    ids = jnp.concatenate([ids[0:1], ids[1:2], jnp.zeros((1, 64), f32)], axis=1)
    columns = []
    for r in range(0, PIECE, 2):
        pair = (part[r * 8 : (r + 1) * 8], part[(r + 1) * 8 : (r + 2) * 8])
        columns += [rows_of[:, :DL] for rows_of in pair] + [rows_of[:, DL:] for rows_of in pair]
    columns += [keys[pl.ds(j, 8, stride=4), :] for j in range(4)]
    columns.append(jnp.where(iota((8, 128), 0) == 0, ids, 0.0))
    chunk = jnp.concatenate(columns, axis=1).astype(bf16)
    for n in range(4):
        z_ref[n] = chunk
    for h in range(IH):
        rows[pl.ds(h, 2, stride=IH), :] = iq_ref[:, h * ID : (h + 1) * ID].astype(f32)
    weights = iw_ref[...].astype(f32)
    weights = jnp.concatenate([weights[0:1], weights[1:2]], axis=1)
    at = iota((16, 128), 0)
    tail = jnp.where(at == 0, weights, jnp.where(at == 1, ids, 0.0)).astype(bf16)
    head = rows[...].astype(bf16)
    for p in range(PLANE):
        y_ref[p, 0 : 2 * IH, :] = head
        y_ref[p, 2 * IH : 2 * IH + 16, :] = tail


def pack(kv_turned, index_keys, index_queries, index_weights, q_blocks):
    return pl.pallas_call(
        pack_kernel,
        out_shape=(
            jax.ShapeDtypeStruct((4, 8, Z_COLS), bf16),
            jax.ShapeDtypeStruct((PLANE, 2 * IH + 16, ID), bf16),
        ),
        in_specs=[main_memory()] * 5,
        out_specs=(whole(), whole()),
        scratch_shapes=[pltpu.VMEM((32, ID), f32), pltpu.VMEM((2 * IH, ID), f32)]
        + [
            pltpu.VMEM(value.shape, value.dtype)
            for value in (kv_turned, index_keys, index_queries, index_weights, q_blocks)
        ]
        + [pltpu.SemaphoreType.DMA((5,))],
        compiler_params=params(60 * 1024 * 1024),
        name="pack",
    )(kv_turned, index_keys, index_queries, index_weights, q_blocks)


def named_columns(span, ids):
    first, count, unused = span
    lane = iota((count, 128), 1)
    named = jnp.zeros((count, 128), f32)
    for n, row in enumerate(ids):
        place = table_row(row) - first
        hit = jnp.where(place == iota((count, row.shape[1]), 0), 1.0, 0.0)
        named = jnp.where(lane == n, jnp.max(hit, axis=1, keepdims=True), named)
    return named


def slot_codes(span, named):
    count = span[1]
    t, u = iota((count, count), 0), iota((count, count), 1)
    before = jnp.where((t // 8 == u // 8) & (u < t), 1.0, 0.0).astype(bf16)
    rank = jnp.dot(before, named.astype(bf16), preferred_element_type=f32)
    return jnp.where(named > 0.5, rank, -1.0)


def slot_keys(span, named):
    code = slot_codes(span, named)
    shard = slot_shard(span, iota((span[1], 1), 0)).astype(f32)
    return jnp.where((code >= 0.0) & (shard >= 0.0), shard * 2.0 + code, -1.0)


def gather_kernel(span, tables, y_ref, scores_ref, out_ref, onehot):
    first, count, slots = span
    rows = [
        y_ref[p, 2 * IH : 2 * IH + 16, :].astype(f32)[1:2, :64].astype(jnp.int32)
        for p in range(PLANE)
    ]
    keys = slot_keys(span, named_columns(span, rows))
    halves = 2 if span is NEAR else 1
    each = halves * slots
    pad = -count % 128
    keys = jnp.concatenate([keys, jnp.zeros((pad, 128), f32)], axis=0)
    keys = jnp.concatenate([keys.T[:PLANE, :count]] * halves, axis=1)
    line, lane = iota((each, halves * count), 0), iota((each, halves * count), 1)
    half = jnp.where(line >= slots, 1, 0)
    there = jnp.where(lane >= count, 1, 0)
    wanted = jnp.where(half == there, line - half * slots, -5).astype(f32)
    picks = [jnp.where(keys[p : p + 1] == wanted, 1.0, 0.0) for p in range(PLANE)]
    onehot[...] = jnp.concatenate(picks, axis=0).astype(bf16)
    columns = KV_COLS // halves
    for c in range(columns // 384):
        rows = [
            ref[:, h * columns + c * 384 : h * columns + (c + 1) * 384]
            for h in range(halves)
            for ref in tables
        ]
        out_ref[:, c * 384 : (c + 1) * 384] = jnp.dot(
            onehot[...], jnp.concatenate(rows, axis=0), preferred_element_type=f32
        ).astype(bf16)
    if scores_ref is not None:
        for p in range(PLANE):
            at = p * each
            out_ref[at : at + 16, columns:] = scores_ref[p]
            out_ref[at + 16 : at + each, columns:] = jnp.zeros((each - 16, 128), bf16)


def gather(name, span, tables, y, afters, scores=None):
    first, count, slots = span

    def body(*refs):
        refs = list(refs)
        held = [refs.pop(0) for table in tables]
        y_ref = refs.pop(0)
        scores_ref = None
        for after in afters:
            refs.pop(0)
        if scores is not None:
            scores_ref = refs.pop(0)
        gather_kernel(span, held, y_ref, scores_ref, *refs)

    halves = 2 if span is NEAR else 1
    operands = [*tables, y, *afters]
    in_specs = [whole()] * (len(tables) + 1) + [anywhere()] * len(afters)
    columns = WIDTH
    if scores is not None:
        operands.append(scores)
        in_specs.append(whole())
        columns = SENT_COLS
    return pl.pallas_call(
        body,
        out_shape=jax.ShapeDtypeStruct((PLANE * halves * slots, columns), bf16),
        in_specs=in_specs,
        out_specs=whole(),
        scratch_shapes=[pltpu.VMEM((PLANE * halves * slots, halves * count), bf16)],
        compiler_params=params(),
        cost_estimate=pl.CostEstimate(
            flops=2 * PLANE * slots * 4 * count * WIDTH,
            bytes_accessed=3_000_000,
            transcendentals=0,
        ),
        name=name,
    )(*operands)


def serve_kernel(kv_ref, *refs):
    tables, outs = refs[:8], refs[9:]
    at = lax.axis_index("ctx")
    level = at // 2
    lines = []
    line = iota((32, 128), 0)
    for away in AWAYS:
        outer = (level + away) % LEVELS // 4
        for other in range(2):
            ref = tables[(0, 1, 3, 2)[away % 4] + 4 * other]
            values = jnp.where(line == outer * 8, ref[:, IDS_AT:].astype(f32), 0.0)
            lines.append(jnp.sum(values, axis=0, keepdims=True))
    lines += [jnp.full((6, 128), -1.0, f32)]
    ids = jnp.concatenate(lines, axis=0)[:, :64]
    own = (at * 8).astype(f32)
    lane = iota((16, 512), 1)
    codes = jnp.full((16, 512), -1.0, f32)
    taken = jnp.zeros((16, 1), f32)
    for b in range(8):
        hit = jnp.max(jnp.where(ids == own + b, 1.0, 0.0), axis=1, keepdims=True)
        codes = jnp.where((lane // BLK == b) & (hit > 0.5), taken, codes)
        taken = taken + hit
    row, lane = iota((64, 512), 0), iota((64, 512), 1)
    kind = (row // 32).astype(f32)
    for n in range(len(AWAYS)):
        select = jnp.concatenate(
            [
                jnp.where(
                    (row % 32 + 32 * half == lane % BLK) & (codes[m : m + 1, :] == kind),
                    1.0,
                    0.0,
                )
                for half in range(2)
                for m in (2 * n, 2 * n + 1)
            ],
            axis=0,
        ).astype(bf16)
        got = lax.dot_general(
            select, kv_ref[...], (((1,), (1,)), ((), ())), preferred_element_type=f32
        )
        got = (got[:128], got[128:])
        columns = [part[:, :DL] for part in got] + [part[:, DL:] for part in got]
        outs[n][...] = jnp.concatenate(columns, axis=1).astype(bf16)


def serve(kv_turned, tables, after):
    return pl.pallas_call(
        serve_kernel,
        out_shape=tuple(jax.ShapeDtypeStruct((2 * BLK, WIDTH), bf16) for away in AWAYS),
        in_specs=[whole()] * 9 + [anywhere()],
        out_specs=(whole(),) * len(AWAYS),
        compiler_params=params(),
        cost_estimate=pl.CostEstimate(
            flops=2 * 10 * 128 * 512 * DQK, bytes_accessed=4_000_000, transcendentals=0
        ),
        name="serve",
    )(kv_turned, *tables, after)


def score_kernel(*refs):
    tables, y_ref, out_ref, keys = refs[:8], refs[8], refs[9], refs[10]
    tail = jnp.concatenate(
        [y_ref[p, 2 * IH : 2 * IH + 16, :].astype(f32)[0:1] for p in range(PLANE)], axis=0
    )
    weights = jnp.concatenate(
        [tail * index_scale, jnp.zeros((128 - PLANE, 128), f32)], axis=0
    ).T
    lane = iota((128, 128), 1)
    at = lax.axis_index("ctx")
    for n, ref in enumerate(tables):
        step = (0, 1, 3, 2)[n % 4]
        inner = (at // 2 + step) % 4
        core = (at + n // 4) % 2
        for outer in range(4):
            shard = (outer * 4 + inner) * 2 + core
            for j in range(4):
                cols = slice(KV_COLS + j * ID, KV_COLS + (j + 1) * ID)
                keys[pl.ds(shard * 32 + j, 8, stride=4), :] = ref[
                    outer * 8 : (outer + 1) * 8, cols
                ].astype(f32)
    key_rows = keys[...].astype(bf16)

    def peers(g, carry):
        products = lax.dot_general(
            y_ref[pl.ds(g * 4, 4), 0 : 2 * IH, :].reshape(8 * IH, ID),
            key_rows,
            (((1,), (1,)), ((), ())),
            preferred_element_type=f32,
        )
        for m in range(4):
            weight = jnp.sum(
                jnp.where(lane == g * 4 + m, weights, 0.0), axis=1, keepdims=True
            )
            active = jnp.maximum(products[m * 2 * IH : (m + 1) * 2 * IH], 0.0) * weight
            lines = []
            for i in range(2):
                total = jnp.sum(active[i * IH : (i + 1) * IH], axis=0, keepdims=True)
                lines += [total[:, c * 128 : (c + 1) * 128] for c in range(8)]
            out_ref[g * 4 + m] = jnp.concatenate(lines, axis=0).astype(bf16)
        return carry

    lax.fori_loop(0, PLANE // 4, peers, 0)


def score(tables, y):
    return pl.pallas_call(
        score_kernel,
        out_shape=jax.ShapeDtypeStruct((PLANE, 16, 128), bf16),
        in_specs=[whole()] * 9,
        out_specs=whole(),
        scratch_shapes=[pltpu.VMEM((1024, ID), f32)],
        compiler_params=params(),
        cost_estimate=pl.CostEstimate(
            flops=2 * 2048 * 128 * 1024, bytes_accessed=2_000_000, transcendentals=0
        ),
        name="score",
    )(*tables, y)


def attend_kernel(q_ref, ids_ref, near_ref, far_ref, *refs):
    count = len(AWAYS)
    mine, crossed = refs[:count], refs[count]
    out_ref, index_ref, scores, total, turned, direct, sem = refs[count + 1 :]
    copies = []
    for n in range(count):
        for other in range(2):
            source = crossed.at[pl.ds(n * 64, 64)] if other else mine[n].at[pl.ds(0, 64)]
            target = direct.at[pl.ds((2 * n + other) * 64, 64)]
            copies.append(pltpu.make_async_copy(source, target, sem.at[2 * n + other]))
    for copy in copies:
        copy.start()
    ctx = lax.axis_index("ctx")
    rank = ctx * PLANE + lax.axis_index("pb")
    ids = ids_ref[...]
    own_block = 240 + rank * 2 // BLK
    own_row = table_row(own_block)
    offsets = [((rank * 2 + i) % BLK).astype(f32) for i in range(2)]
    query = jnp.concatenate([q_ref[0], q_ref[1]], axis=0)
    latent = query[:, :DL]
    rotary = query[:, DL:]
    nothing = jnp.zeros_like(rotary)
    padded = (
        jnp.concatenate([latent, rotary, nothing], axis=1),
        jnp.concatenate([latent, nothing, rotary], axis=1),
    )
    contract = (((1,), (1,)), ((), ()))
    sets = []
    filled = [0]
    tops = [jnp.full((HEADS, 128), -1e30, f32) for i in range(2)]

    def keep(block, place, limits, values):
        at, width = filled[0], block.shape[1]
        for i in range(2):
            heads = slice(i * HEADS, (i + 1) * HEADS)
            value = jnp.where(place < limits[i], block[heads], -1e30)
            scores[heads, at : at + width] = value
            for k in range(0, width, 128):
                tops[i] = jnp.maximum(tops[i], value[:, k : k + 128])
        sets.append((at, width, values))
        filled[0] += width

    def product(left, right):
        return lax.dot_general(left, right, contract, preferred_element_type=f32)

    for span, ref, step in ((NEAR, near_ref, 384), (FAR, far_ref, 256)):
        first, count, slots = span
        one, two = named_columns(span, [ids[0:1]]), named_columns(span, [ids[1:2]])
        members = (one[:, 0:1], two[:, 0:1])
        keys = slot_keys(span, jnp.maximum(one, two))[:, 0:1]
        halves = 2 if span is NEAR else 1
        width = PLANE * halves * slots
        line = iota((count, 128), 0)
        chosen = keys == (iota((1, width), 1) % slots).astype(f32)
        limits = []
        for i in range(2):
            limit = jnp.where(line[:, 0:1] + first == own_row, offsets[i], 63.0) + 1.0
            limit = jnp.where(members[i] > 0.5, limit, 0.0)
            limits.append(jnp.sum(jnp.where(chosen, limit, 0.0), axis=0, keepdims=True))
        lane = iota((1, width), 1)
        place = lane // (halves * slots) * PIECE
        if halves == 2:
            place = place + lane // slots % 2 * 2
        for k in range(width // step):
            rows = slice(k * step, (k + 1) * step)
            for r in range(PIECE // halves):
                half, parity = r // 2, r % 2
                at = half * WIDTH + parity * DL
                columns = slice(at, at + DL)
                turn = half * WIDTH + 2 * DL
                block = product(
                    padded[parity],
                    jnp.concatenate([ref[rows, columns], ref[rows, turn : turn + 128]], axis=1),
                )
                keep(
                    block,
                    (place[:, rows] + r).astype(f32),
                    [limit[:, rows] for limit in limits],
                    [(ref, rows, columns)],
                )

    count = 16 * len(AWAYS)
    line = iota((count, 128), 0)
    lane = iota((count, 128), 1)
    named = jnp.zeros((count, 128), f32)
    shard = ids // 8
    away = (shard // 2 - ctx // 2 + LEVELS) % LEVELS
    turn = jnp.where(away < 3, away, jnp.where(away > 13, away - 11, -8))
    place = (turn * 2 + (shard + ctx) % 2) * 8 + ids % 8
    own_away = (own_block // 16 - ctx // 2 + LEVELS) % LEVELS
    own_turn = jnp.where(own_away < 3, own_away, jnp.where(own_away > 13, own_away - 11, -8))
    own_place = (own_turn * 2 + (own_block // 8 + ctx) % 2) * 8 + own_block % 8
    for i in range(2):
        hit = jnp.where(place[i : i + 1] == iota((count, ids.shape[1]), 0), 1.0, 0.0)
        named = jnp.where(lane == i, jnp.max(hit, axis=1, keepdims=True), named)
    members = named
    named = jnp.maximum(named[:, 0:1], named[:, 1:2])
    code = slot_codes((0, count, 2), jnp.broadcast_to(named, (count, 128)))
    chosen = code == (lane // 32 % 2).astype(f32)
    limits = []
    for i in range(2):
        limit = jnp.where(line[:, 0:1] == own_place, offsets[i], 63.0) + 1.0
        limit = jnp.where(members[:, i : i + 1] > 0.5, limit, 0.0)
        limits.append(jnp.where(chosen, limit, 0.0))
    low = iota((1, 128), 1) < 64
    shown = [
        [
            jnp.where(
                low,
                jnp.sum(limit[n * 8 : (n + 1) * 8], axis=0, keepdims=True),
                jnp.sum(limit[(n + 1) * 8 : (n + 2) * 8], axis=0, keepdims=True),
            )
            for n in range(0, 2 * len(AWAYS), 2)
        ]
        for limit in limits
    ]
    here = iota((1, 128), 1) % 32
    for copy in copies:
        copy.wait()
    for first, last in ((0, 2), (2, 4), (4, 5)):
        rows = slice(first * 128, last * 128)
        for parity in range(2):
            columns = slice(parity * DL, (parity + 1) * DL)
            block = product(
                padded[parity],
                jnp.concatenate(
                    [direct[rows, columns], direct[rows, 2 * DL : 2 * DL + 128]], axis=1
                ),
            )
            keep(
                block,
                jnp.concatenate([(here + 32 * parity).astype(f32)] * (last - first), axis=1),
                [jnp.concatenate(each[first:last], axis=1) for each in shown],
                [(direct, rows, columns)],
            )

    highest = jnp.max(jnp.concatenate(tops, axis=0), axis=1, keepdims=True)
    norm = jnp.zeros((2 * HEADS, 128), f32)
    for c in range(32):
        cols = slice(c * 128, (c + 1) * 128)
        weight = jnp.exp((scores[:, cols] - highest) * score_scale)
        scores[:, cols] = weight
        norm = norm + weight
    norm = jnp.sum(norm, axis=1, keepdims=True)
    share = 1.0 / norm
    for c, (at, width, values) in enumerate(sets):
        probs = (scores[:, at : at + width] * share).astype(bf16)
        rows = [ref[rows, columns] for ref, rows, columns in values]
        rows = rows[0] if len(rows) == 1 else jnp.concatenate(rows, axis=0)
        term = jnp.dot(probs, rows, preferred_element_type=f32)
        for k in range(4):
            if c == 0:
                total[k] = term[:, k * 128 : (k + 1) * 128]
            else:
                total[k] += term[:, k * 128 : (k + 1) * 128]
    for h in range(HEADS):
        for k in range(4):
            at = h * DL + k * 128
            out_ref[:, at : at + 128] = total[k, pl.ds(h, 2, stride=HEADS), :].astype(bf16)

    tiles = [
        far_ref[p * FAR[2] : p * FAR[2] + 16, KV_COLS:].astype(f32)
        for p in range(PLANE)
    ]
    group = iota((16, 128), 1) // 32
    for c in range(4):
        for m in range(4):
            mixed = tiles[4 * m]
            for k in range(4):
                tile = tiles[4 * m + k]
                if k != c:
                    tile = pltpu.roll(tile, (k - c) * 32 % 128, 1)
                mixed = tile if k == 0 else jnp.where(group == k, tile, mixed)
            turned[(c * 4 + m) * 16 : (c * 4 + m + 1) * 16, :] = mixed
            for t in range(8):
                at = (t * 4 + c) * 512 + m * 128
                index_ref[:, at : at + 128] = turned[
                    pl.ds((c * 4 + m) * 16 + t, 2, stride=8), :
                ].astype(bf16)


def attend(query, ids, near, far, mine, crossed):
    return pl.pallas_call(
        attend_kernel,
        out_shape=(
            jax.ShapeDtypeStruct((2, HEADS * DL), bf16),
            jax.ShapeDtypeStruct((2, 16384), bf16),
        ),
        in_specs=[whole()] * 4 + [main_memory()] * (1 + len(mine)),
        out_specs=(whole(), whole()),
        scratch_shapes=[
            pltpu.VMEM((2 * HEADS, 4096), f32),
            pltpu.VMEM((4, 2 * HEADS, 128), f32),
            pltpu.VMEM((256, 128), f32),
            pltpu.VMEM((128 * len(AWAYS), WIDTH), bf16),
            pltpu.SemaphoreType.DMA((2 * len(AWAYS),)),
        ],
        compiler_params=params(),
        cost_estimate=pl.CostEstimate(
            flops=2 * 256 * 4096 * 1152, bytes_accessed=6_000_000, transcendentals=256 * 4096
        ),
        name="attend",
    )(query, ids, near, far, *mine, crossed)


def two_levels_on(value):
    pairs = [
        ((level + (2, -2)[core]) % LEVELS * 2 + core, level * 2 + core)
        for level in range(LEVELS)
        for core in range(2)
    ]
    return lax.ppermute(value, "ctx", pairs)


def tie_kernel(value_ref, after_ref, out_ref):
    pass


def tie(value, after):
    return pl.pallas_call(
        tie_kernel,
        out_shape=jax.ShapeDtypeStruct(value.shape, value.dtype),
        in_specs=[anywhere(), anywhere()],
        out_specs=anywhere(),
        input_output_aliases={0: 0},
        name="tie",
    )(value, after)


def join_kernel(*refs):
    out_ref = refs[-1]
    for n, ref in enumerate(refs[:-1]):
        out_ref[n * 64 : (n + 1) * 64, :] = ref[64:, :]


def join(parts):
    return pl.pallas_call(
        join_kernel,
        out_shape=jax.ShapeDtypeStruct((len(parts) * 64, WIDTH), bf16),
        in_specs=[whole()] * len(parts),
        out_specs=whole(),
        compiler_params=params(),
        cost_estimate=pl.CostEstimate(flops=0, bytes_accessed=2_000_000, transcendentals=0),
        name="join",
    )(*parts)


def level_from(value, away):
    pairs = [
        ((level + away) % LEVELS * 2 + core, level * 2 + core)
        for level in range(LEVELS)
        for core in range(2)
    ]
    return lax.ppermute(value, "ctx", pairs)


def swap(value):
    return lax.ppermute(value, "ctx", [(at, at ^ 1) for at in range(2 * LEVELS)])


def exchange(rows):
    parts = rows.reshape(PLANE, rows.shape[0] // PLANE, rows.shape[1])
    got = lax.all_to_all(parts, "pb", split_axis=0, concat_axis=0, tiled=True)
    return got.reshape(rows.shape)


def outer_levels(chunks):
    groups = [
        [(outer * 4 + inner) * 2 + core for outer in range(4)]
        for inner in range(4)
        for core in range(2)
    ]
    got = lax.all_to_all(
        chunks, "ctx", split_axis=0, concat_axis=0, axis_index_groups=groups, tiled=True
    )
    return got.reshape(chunks.shape[0] * chunks.shape[1], chunks.shape[2])


def local(q_latent, kv_cache, index_queries, index_weights, index_keys, q_blocks):
    kv_turned = kv_cache.T
    z, y = pack(kv_turned, index_keys, index_queries, index_weights, q_blocks)
    held = outer_levels(z)
    y = lax.all_to_all(y, "pb", split_axis=0, concat_axis=0, tiled=True)
    across = swap(held)
    others = [level_from(held, 1), level_from(held, 15), two_levels_on(held)]
    near = exchange(gather("near", NEAR, [held, across], y, others))
    swapped = [swap(other) for other in others]
    tables = [held] + others + [across] + swapped
    scores = score(tables, y)
    sent = gather("far", FAR, others + swapped, y, [], scores)
    served = serve(kv_turned, tables, sent)
    far = exchange(tie(sent, near))
    mine = [served[0]]
    for away in AWAYS[1:]:
        mine.append(level_from(served[AWAYS.index(-away % LEVELS)], away))
    crossed = swap(join(mine))
    query = q_latent.reshape(2, HEADS, DQK)
    return tuple(attend(query, q_blocks, near, far, mine, crossed))


def solution(mesh):
    in_specs = (
        P(("ctx", "pb"), None),
        P("ctx", None),
        P(("ctx", "pb"), None),
        P(("ctx", "pb"), None),
        P(("ctx", "pb"), None),
        P(("ctx", "pb"), None),
    )
    out_specs = (P(("ctx", "pb"), None), P(("ctx", "pb"), None))
    return jax.shard_map(local, mesh=mesh, in_specs=in_specs, out_specs=out_specs, check_vma=False)
```

```python
import jax
import jax.numpy as jnp
from jax import lax
from jax.experimental import pallas as pl
from jax.experimental.pallas import tpu as pltpu
from jax.sharding import PartitionSpec as P

DL = 512
DQK = 576
ROT = DQK - DL
BLK = 64
IH = 64
ID = 128
HEADS = 128
PLANE = 16
LEVELS = 16
PIECE = BLK // PLANE
KV_COLS = PIECE * DQK
WIDTH = KV_COLS // 2
IDS_AT = KV_COLS + 4 * ID
Z_COLS = IDS_AT + 128
SENT_COLS = KV_COLS + 128
AWAYS = (0, 1, 2, 14, 15)
VMEM_LIMIT = 24 * 1024 * 1024

score_scale = 192.0 ** (-0.5)
index_scale = 128.0 ** (-0.5)
f32 = jnp.float32
bf16 = jnp.bfloat16

NEAR = (0, 64, 12)
FAR = (64, 192, 32)


def params(limit=VMEM_LIMIT):
    return pltpu.CompilerParams(vmem_limit_bytes=limit)


def whole():
    return pl.BlockSpec(memory_space=pltpu.VMEM)


def anywhere():
    return pl.BlockSpec(memory_space=pl.ANY)


def main_memory():
    return pl.BlockSpec(memory_space=pltpu.HBM)


def iota(shape, dim):
    return lax.broadcasted_iota(jnp.int32, shape, dim)


def table_row(block):
    at = lax.axis_index("ctx")
    half = (block // 8 + at) % 2
    turn = (block // 16 - at // 2 + LEVELS) % 4
    order = jnp.where(turn == 3, 2, jnp.where(turn == 2, 3, turn))
    inner = block // 64 * 8 + block % 8
    return jnp.where(
        order == 0, half * 32 + inner, 64 + half * 96 + (order - 1) * 32 + inner
    )


def slot_shard(span, t):
    level = lax.axis_index("ctx") // 2
    if span is NEAR:
        away = (t % 32 // 8 * 4 + level % 4 - level + LEVELS) % LEVELS
        return jnp.where(away == 0, -1, t // 32 * 3 + away // 4 - 1)
    order = t % 96 // 32
    step = jnp.where(order == 0, 1, jnp.where(order == 1, 3, 2))
    away = (t % 32 // 8 * 4 + (level + step) % 4 - level + LEVELS) % LEVELS
    which = jnp.where(order == 1, away // 4, away // 4 - 1)
    return jnp.where((away > 2) & (away < 14), t // 96 * 8 + order * 3 + which, -1)


def pack_kernel(*refs):
    sources, (z_ref, y_ref, keys, rows), targets, sem = refs[:5], refs[5:9], refs[9:14], refs[14]
    copies = [
        pltpu.make_async_copy(source, target, sem.at[n])
        for n, (source, target) in enumerate(zip(sources, targets))
    ]
    for copy in copies:
        copy.start()
    for copy in copies:
        copy.wait()
    kv_ref, ik_ref, iq_ref, iw_ref, qb_ref = targets
    piece = lax.axis_index("pb")
    shard_keys = kv_ref.shape[1]
    line = iota((PIECE * 8, shard_keys), 0)
    source = (line % 8) * BLK + piece * PIECE + line // 8
    select = jnp.where(source == iota(source.shape, 1), 1.0, 0.0).astype(bf16)
    part = lax.dot_general(
        select, kv_ref[...], (((1,), (1,)), ((), ())), preferred_element_type=f32
    )
    keys[...] = ik_ref[...].astype(f32)
    ids = qb_ref[...].astype(f32)
    ids = jnp.concatenate([ids[0:1], ids[1:2], jnp.zeros((1, 64), f32)], axis=1)
    columns = []
    for r in range(0, PIECE, 2):
        pair = (part[r * 8 : (r + 1) * 8], part[(r + 1) * 8 : (r + 2) * 8])
        columns += [rows_of[:, :DL] for rows_of in pair] + [rows_of[:, DL:] for rows_of in pair]
    columns += [keys[pl.ds(j, 8, stride=4), :] for j in range(4)]
    columns.append(jnp.where(iota((8, 128), 0) == 0, ids, 0.0))
    chunk = jnp.concatenate(columns, axis=1).astype(bf16)
    for n in range(4):
        z_ref[n] = chunk
    for h in range(IH):
        rows[pl.ds(h, 2, stride=IH), :] = iq_ref[:, h * ID : (h + 1) * ID].astype(f32)
    weights = iw_ref[...].astype(f32)
    weights = jnp.concatenate([weights[0:1], weights[1:2]], axis=1)
    at = iota((16, 128), 0)
    tail = jnp.where(at == 0, weights, jnp.where(at == 1, ids, 0.0)).astype(bf16)
    head = rows[...].astype(bf16)
    for p in range(PLANE):
        y_ref[p, 0 : 2 * IH, :] = head
        y_ref[p, 2 * IH : 2 * IH + 16, :] = tail


def pack(kv_turned, index_keys, index_queries, index_weights, q_blocks):
    return pl.pallas_call(
        pack_kernel,
        out_shape=(
            jax.ShapeDtypeStruct((4, 8, Z_COLS), bf16),
            jax.ShapeDtypeStruct((PLANE, 2 * IH + 16, ID), bf16),
        ),
        in_specs=[main_memory()] * 5,
        out_specs=(whole(), whole()),
        scratch_shapes=[pltpu.VMEM((32, ID), f32), pltpu.VMEM((2 * IH, ID), f32)]
        + [
            pltpu.VMEM(value.shape, value.dtype)
            for value in (kv_turned, index_keys, index_queries, index_weights, q_blocks)
        ]
        + [pltpu.SemaphoreType.DMA((5,))],
        compiler_params=params(60 * 1024 * 1024),
        name="pack",
    )(kv_turned, index_keys, index_queries, index_weights, q_blocks)


def named_columns(span, ids):
    first, count, unused = span
    lane = iota((count, 128), 1)
    named = jnp.zeros((count, 128), f32)
    for n, row in enumerate(ids):
        place = table_row(row) - first
        hit = jnp.where(place == iota((count, row.shape[1]), 0), 1.0, 0.0)
        named = jnp.where(lane == n, jnp.max(hit, axis=1, keepdims=True), named)
    return named


def slot_codes(span, named):
    count = span[1]
    t, u = iota((count, count), 0), iota((count, count), 1)
    before = jnp.where((t // 8 == u // 8) & (u < t), 1.0, 0.0).astype(bf16)
    rank = jnp.dot(before, named.astype(bf16), preferred_element_type=f32)
    return jnp.where(named > 0.5, rank, -1.0)


def slot_keys(span, named):
    code = slot_codes(span, named)
    shard = slot_shard(span, iota((span[1], 1), 0)).astype(f32)
    return jnp.where((code >= 0.0) & (shard >= 0.0), shard * 2.0 + code, -1.0)


def gather_kernel(span, tables, y_ref, scores_ref, out_ref, onehot):
    first, count, slots = span
    rows = [
        y_ref[p, 2 * IH : 2 * IH + 16, :].astype(f32)[1:2, :64].astype(jnp.int32)
        for p in range(PLANE)
    ]
    keys = slot_keys(span, named_columns(span, rows))
    halves = 2 if span is NEAR else 1
    each = halves * slots
    pad = -count % 128
    keys = jnp.concatenate([keys, jnp.zeros((pad, 128), f32)], axis=0)
    keys = jnp.concatenate([keys.T[:PLANE, :count]] * halves, axis=1)
    line, lane = iota((each, halves * count), 0), iota((each, halves * count), 1)
    half = jnp.where(line >= slots, 1, 0)
    there = jnp.where(lane >= count, 1, 0)
    wanted = jnp.where(half == there, line - half * slots, -5).astype(f32)
    picks = [jnp.where(keys[p : p + 1] == wanted, 1.0, 0.0) for p in range(PLANE)]
    onehot[...] = jnp.concatenate(picks, axis=0).astype(bf16)
    columns = KV_COLS // halves
    for c in range(columns // 384):
        rows = [
            ref[:, h * columns + c * 384 : h * columns + (c + 1) * 384]
            for h in range(halves)
            for ref in tables
        ]
        out_ref[:, c * 384 : (c + 1) * 384] = jnp.dot(
            onehot[...], jnp.concatenate(rows, axis=0), preferred_element_type=f32
        ).astype(bf16)
    if scores_ref is not None:
        for p in range(PLANE):
            at = p * each
            out_ref[at : at + 16, columns:] = scores_ref[p]
            out_ref[at + 16 : at + each, columns:] = jnp.zeros((each - 16, 128), bf16)


def gather(name, span, tables, y, afters, scores=None):
    first, count, slots = span

    def body(*refs):
        refs = list(refs)
        held = [refs.pop(0) for table in tables]
        y_ref = refs.pop(0)
        scores_ref = None
        for after in afters:
            refs.pop(0)
        if scores is not None:
            scores_ref = refs.pop(0)
        gather_kernel(span, held, y_ref, scores_ref, *refs)

    halves = 2 if span is NEAR else 1
    operands = [*tables, y, *afters]
    in_specs = [whole()] * (len(tables) + 1) + [anywhere()] * len(afters)
    columns = WIDTH
    if scores is not None:
        operands.append(scores)
        in_specs.append(whole())
        columns = SENT_COLS
    return pl.pallas_call(
        body,
        out_shape=jax.ShapeDtypeStruct((PLANE * halves * slots, columns), bf16),
        in_specs=in_specs,
        out_specs=whole(),
        scratch_shapes=[pltpu.VMEM((PLANE * halves * slots, halves * count), bf16)],
        compiler_params=params(),
        cost_estimate=pl.CostEstimate(
            flops=2 * PLANE * slots * 4 * count * WIDTH,
            bytes_accessed=3_000_000,
            transcendentals=0,
        ),
        name=name,
    )(*operands)


def serve_kernel(kv_ref, ids_ref, after_ref, *outs):
    at = lax.axis_index("ctx")
    ids = ids_ref[:, :64]
    own = (at * 8).astype(f32)
    lane = iota((16, 512), 1)
    codes = jnp.full((16, 512), -1.0, f32)
    taken = jnp.zeros((16, 1), f32)
    for b in range(8):
        hit = jnp.max(jnp.where(ids == own + b, 1.0, 0.0), axis=1, keepdims=True)
        codes = jnp.where((lane // BLK == b) & (hit > 0.5), taken, codes)
        taken = taken + hit
    row, lane = iota((64, 512), 0), iota((64, 512), 1)
    kind = (row // 32).astype(f32)
    for n in range(len(AWAYS)):
        select = jnp.concatenate(
            [
                jnp.where(
                    (row % 32 + 32 * half == lane % BLK) & (codes[m : m + 1, :] == kind),
                    1.0,
                    0.0,
                )
                for half in range(2)
                for m in (2 * n, 2 * n + 1)
            ],
            axis=0,
        ).astype(bf16)
        got = lax.dot_general(
            select, kv_ref[...], (((1,), (1,)), ((), ())), preferred_element_type=f32
        )
        got = (got[:128], got[128:])
        columns = [part[:, :DL] for part in got] + [part[:, DL:] for part in got]
        outs[n][...] = jnp.concatenate(columns, axis=1).astype(bf16)


def serve(kv_turned, ids, after):
    return pl.pallas_call(
        serve_kernel,
        out_shape=tuple(jax.ShapeDtypeStruct((2 * BLK, WIDTH), bf16) for away in AWAYS),
        in_specs=[whole()] * 2 + [anywhere()],
        out_specs=(whole(),) * len(AWAYS),
        compiler_params=params(),
        cost_estimate=pl.CostEstimate(
            flops=2 * 10 * 128 * 512 * DQK, bytes_accessed=4_000_000, transcendentals=0
        ),
        name="serve",
    )(kv_turned, ids, after)


def score_kernel(*refs):
    tables, (y_ref, out_ref, ids_ref, keys) = refs[:8], refs[8:]
    tail = jnp.concatenate(
        [y_ref[p, 2 * IH : 2 * IH + 16, :].astype(f32)[0:1] for p in range(PLANE)], axis=0
    )
    weights = jnp.concatenate(
        [tail * index_scale, jnp.zeros((128 - PLANE, 128), f32)], axis=0
    ).T
    at = lax.axis_index("ctx")
    level = at // 2
    lines = []
    line = iota((32, 128), 0)
    for away in AWAYS:
        outer = (level + away) % LEVELS // 4
        for other in range(2):
            ref = tables[(0, 1, 3, 2)[away % 4] + 4 * other]
            values = jnp.where(line == outer * 8, ref[:, IDS_AT:].astype(f32), 0.0)
            lines.append(jnp.sum(values, axis=0, keepdims=True))
    lines += [jnp.full((6, 128), -1.0, f32)]
    ids_ref[...] = jnp.concatenate(lines, axis=0)
    lane = iota((128, 128), 1)
    for n, ref in enumerate(tables):
        step = (0, 1, 3, 2)[n % 4]
        inner = (at // 2 + step) % 4
        core = (at + n // 4) % 2
        for outer in range(4):
            shard = (outer * 4 + inner) * 2 + core
            for j in range(4):
                cols = slice(KV_COLS + j * ID, KV_COLS + (j + 1) * ID)
                keys[pl.ds(shard * 32 + j, 8, stride=4), :] = ref[
                    outer * 8 : (outer + 1) * 8, cols
                ].astype(f32)
    key_rows = keys[...].astype(bf16)

    def peers(g, carry):
        products = lax.dot_general(
            y_ref[pl.ds(g * 4, 4), 0 : 2 * IH, :].reshape(8 * IH, ID),
            key_rows,
            (((1,), (1,)), ((), ())),
            preferred_element_type=f32,
        )
        for m in range(4):
            weight = jnp.sum(
                jnp.where(lane == g * 4 + m, weights, 0.0), axis=1, keepdims=True
            )
            active = jnp.maximum(products[m * 2 * IH : (m + 1) * 2 * IH], 0.0) * weight
            lines = []
            for i in range(2):
                total = jnp.sum(active[i * IH : (i + 1) * IH], axis=0, keepdims=True)
                lines += [total[:, c * 128 : (c + 1) * 128] for c in range(8)]
            out_ref[g * 4 + m] = jnp.concatenate(lines, axis=0).astype(bf16)
        return carry

    lax.fori_loop(0, PLANE // 4, peers, 0)


def score(tables, y):
    return pl.pallas_call(
        score_kernel,
        out_shape=(
            jax.ShapeDtypeStruct((PLANE, 16, 128), bf16),
            jax.ShapeDtypeStruct((16, 128), f32),
        ),
        in_specs=[whole()] * 9,
        out_specs=(whole(), whole()),
        scratch_shapes=[pltpu.VMEM((1024, ID), f32)],
        compiler_params=params(),
        cost_estimate=pl.CostEstimate(
            flops=2 * 2048 * 128 * 1024, bytes_accessed=2_000_000, transcendentals=0
        ),
        name="score",
    )(*tables, y)


def product(left, right):
    return lax.dot_general(
        left, right, (((1,), (1,)), ((), ())), preferred_element_type=f32
    )


def attend_start(q_ref, scores):
    ctx = lax.axis_index("ctx")
    rank = ctx * PLANE + lax.axis_index("pb")
    own_block = 240 + rank * 2 // BLK
    offsets = [((rank * 2 + i) % BLK).astype(f32) for i in range(2)]
    query = jnp.concatenate([q_ref[0], q_ref[1]], axis=0)
    latent, rotary = query[:, :DL], query[:, DL:]
    nothing = jnp.zeros_like(rotary)
    padded = (
        jnp.concatenate([latent, rotary, nothing], axis=1),
        jnp.concatenate([latent, nothing, rotary], axis=1),
    )
    sets = []
    filled = [0]
    tops = [jnp.full((HEADS, 128), -1e30, f32) for i in range(2)]

    def keep(block, place, limits, values):
        at, width = filled[0], block.shape[1]
        for i in range(2):
            heads = slice(i * HEADS, (i + 1) * HEADS)
            value = jnp.where(place < limits[i], block[heads], -1e30)
            scores[heads, at : at + width] = value
            for k in range(0, width, 128):
                tops[i] = jnp.maximum(tops[i], value[:, k : k + 128])
        sets.append((at, width, values))
        filled[0] += width

    return ctx, own_block, offsets, padded, sets, tops, keep


def attend_sum(scores, sets, highest, norm, total, fresh):
    for at, width, values in sets:
        weight = jnp.exp((scores[:, at : at + width] - highest) * score_scale)
        for k in range(0, width, 128):
            norm = norm + weight[:, k : k + 128]
        rows = [ref[rows, columns] for ref, rows, columns in values]
        rows = rows[0] if len(rows) == 1 else jnp.concatenate(rows, axis=0)
        term = jnp.dot(weight.astype(bf16), rows, preferred_element_type=f32)
        for k in range(4):
            if fresh:
                total[k] = term[:, k * 128 : (k + 1) * 128]
            else:
                total[k] += term[:, k * 128 : (k + 1) * 128]
        fresh = False
    return norm


def plane_kernel(q_ref, ids_ref, near_ref, far_ref, total, state, index_ref, scores, turned):
    ctx, own_block, offsets, padded, sets, tops, keep = attend_start(q_ref, scores)
    ids = ids_ref[...]
    own_row = table_row(own_block)
    for span, ref, step in ((NEAR, near_ref, 384), (FAR, far_ref, 256)):
        first, count, slots = span
        one, two = named_columns(span, [ids[0:1]]), named_columns(span, [ids[1:2]])
        members = (one[:, 0:1], two[:, 0:1])
        keys = slot_keys(span, jnp.maximum(one, two))[:, 0:1]
        halves = 2 if span is NEAR else 1
        width = PLANE * halves * slots
        line = iota((count, 128), 0)
        chosen = keys == (iota((1, width), 1) % slots).astype(f32)
        limits = []
        for i in range(2):
            limit = jnp.where(line[:, 0:1] + first == own_row, offsets[i], 63.0) + 1.0
            limit = jnp.where(members[i] > 0.5, limit, 0.0)
            limits.append(jnp.sum(jnp.where(chosen, limit, 0.0), axis=0, keepdims=True))
        lane = iota((1, width), 1)
        place = lane // (halves * slots) * PIECE
        if halves == 2:
            place = place + lane // slots % 2 * 2
        for k in range(width // step):
            rows = slice(k * step, (k + 1) * step)
            for r in range(PIECE // halves):
                half, parity = r // 2, r % 2
                at = half * WIDTH + parity * DL
                columns = slice(at, at + DL)
                turn = half * WIDTH + 2 * DL
                block = product(
                    padded[parity],
                    jnp.concatenate([ref[rows, columns], ref[rows, turn : turn + 128]], axis=1),
                )
                keep(
                    block,
                    (place[:, rows] + r).astype(f32),
                    [limit[:, rows] for limit in limits],
                    [(ref, rows, columns)],
                )

    highest = jnp.max(jnp.concatenate(tops, axis=0), axis=1, keepdims=True)
    norm = jnp.zeros((2 * HEADS, 128), f32)
    state[0] = jnp.broadcast_to(highest, (2 * HEADS, 128))
    state[1] = attend_sum(scores, sets, highest, norm, total, True)

    tiles = [
        far_ref[p * FAR[2] : p * FAR[2] + 16, KV_COLS:].astype(f32)
        for p in range(PLANE)
    ]
    group = iota((16, 128), 1) // 32
    for c in range(4):
        for m in range(4):
            mixed = tiles[4 * m]
            for k in range(4):
                tile = tiles[4 * m + k]
                if k != c:
                    tile = pltpu.roll(tile, (k - c) * 32 % 128, 1)
                mixed = tile if k == 0 else jnp.where(group == k, tile, mixed)
            turned[(c * 4 + m) * 16 : (c * 4 + m + 1) * 16, :] = mixed
            for t in range(8):
                at = (t * 4 + c) * 512 + m * 128
                index_ref[:, at : at + 128] = turned[
                    pl.ds((c * 4 + m) * 16 + t, 2, stride=8), :
                ].astype(bf16)


def column_kernel(q_ref, ids_ref, before, state, *refs):
    count = len(AWAYS)
    mine, crossed, (out_ref, scores, total) = refs[:count], refs[count], refs[count + 1 :]
    ctx, own_block, offsets, padded, sets, tops, keep = attend_start(q_ref, scores)
    ids = ids_ref[...]
    count = 16 * len(AWAYS)
    line = iota((count, 128), 0)
    lane = iota((count, 128), 1)
    named = jnp.zeros((count, 128), f32)
    shard = ids // 8
    away = (shard // 2 - ctx // 2 + LEVELS) % LEVELS
    turn = jnp.where(away < 3, away, jnp.where(away > 13, away - 11, -8))
    place = (turn * 2 + (shard + ctx) % 2) * 8 + ids % 8
    own_away = (own_block // 16 - ctx // 2 + LEVELS) % LEVELS
    own_turn = jnp.where(own_away < 3, own_away, jnp.where(own_away > 13, own_away - 11, -8))
    own_place = (own_turn * 2 + (own_block // 8 + ctx) % 2) * 8 + own_block % 8
    for i in range(2):
        hit = jnp.where(place[i : i + 1] == iota((count, ids.shape[1]), 0), 1.0, 0.0)
        named = jnp.where(lane == i, jnp.max(hit, axis=1, keepdims=True), named)
    members = named
    named = jnp.maximum(named[:, 0:1], named[:, 1:2])
    code = slot_codes((0, count, 2), jnp.broadcast_to(named, (count, 128)))
    chosen = code == (lane // 32 % 2).astype(f32)
    limits = []
    for i in range(2):
        limit = jnp.where(line[:, 0:1] == own_place, offsets[i], 63.0) + 1.0
        limit = jnp.where(members[:, i : i + 1] > 0.5, limit, 0.0)
        limits.append(jnp.where(chosen, limit, 0.0))
    low = iota((1, 128), 1) < 64
    shown = [
        [
            jnp.where(
                low,
                jnp.sum(limit[n * 8 : (n + 1) * 8], axis=0, keepdims=True),
                jnp.sum(limit[(n + 1) * 8 : (n + 2) * 8], axis=0, keepdims=True),
            )
            for n in range(0, 2 * len(AWAYS), 2)
        ]
        for limit in limits
    ]
    here = iota((1, 128), 1) % 32
    direct = []
    for n in range(len(AWAYS)):
        direct += [(mine[n], slice(0, 64)), (crossed, slice(n * 64, (n + 1) * 64))]
    for first, last in ((0, 2), (2, 4), (4, 5)):
        parts = direct[2 * first : 2 * last]
        turns = [ref[rows, 2 * DL : 2 * DL + 128] for ref, rows in parts]
        for parity in range(2):
            columns = slice(parity * DL, (parity + 1) * DL)
            values = [ref[rows, columns] for ref, rows in parts]
            both = [jnp.concatenate(pair, axis=1) for pair in zip(values, turns)]
            keep(
                product(padded[parity], jnp.concatenate(both, axis=0)),
                jnp.concatenate([(here + 32 * parity).astype(f32)] * (last - first), axis=1),
                [jnp.concatenate(each[first:last], axis=1) for each in shown],
                [(ref, rows, columns) for ref, rows in parts],
            )

    highest = jnp.max(jnp.concatenate(tops, axis=0), axis=1, keepdims=True)
    highest = jnp.maximum(highest, state[0][:, 0:1])
    fade = jnp.exp((state[0] - highest) * score_scale)
    for k in range(4):
        total[k] = before[k] * fade
    norm = attend_sum(scores, sets, highest, state[1] * fade, total, False)
    share = 1.0 / jnp.sum(norm, axis=1, keepdims=True)
    for k in range(4):
        total[k] = total[k] * share
    for h in range(HEADS):
        for k in range(4):
            at = h * DL + k * 128
            out_ref[:, at : at + 128] = total[k, pl.ds(h, 2, stride=HEADS), :].astype(bf16)


def attend_plane(query, ids, near, far):
    return pl.pallas_call(
        plane_kernel,
        out_shape=(
            jax.ShapeDtypeStruct((4, 2 * HEADS, 128), f32),
            jax.ShapeDtypeStruct((2, 2 * HEADS, 128), f32),
            jax.ShapeDtypeStruct((2, 16384), bf16),
        ),
        in_specs=[whole()] * 4,
        out_specs=(whole(),) * 3,
        scratch_shapes=[
            pltpu.VMEM((2 * HEADS, 2816), f32),
            pltpu.VMEM((256, 128), f32),
        ],
        compiler_params=params(),
        cost_estimate=pl.CostEstimate(
            flops=2 * 256 * 2816 * 1152, bytes_accessed=4_000_000, transcendentals=256 * 2816
        ),
        name="attend_plane",
    )(query, ids, near, far)


def attend_column(query, ids, before, state, mine, crossed):
    return pl.pallas_call(
        column_kernel,
        out_shape=jax.ShapeDtypeStruct((2, HEADS * DL), bf16),
        in_specs=[whole()] * (5 + len(mine)),
        out_specs=whole(),
        scratch_shapes=[
            pltpu.VMEM((2 * HEADS, 1280), f32),
            pltpu.VMEM((4, 2 * HEADS, 128), f32),
        ],
        compiler_params=params(),
        cost_estimate=pl.CostEstimate(
            flops=2 * 256 * 1280 * 1152, bytes_accessed=3_000_000, transcendentals=256 * 1280
        ),
        name="attend_column",
    )(query, ids, before, state, *mine, crossed)


def two_levels_on(value):
    pairs = [
        ((level + (2, -2)[core]) % LEVELS * 2 + core, level * 2 + core)
        for level in range(LEVELS)
        for core in range(2)
    ]
    return lax.ppermute(value, "ctx", pairs)


def tie_kernel(value_ref, after_ref, out_ref):
    pass


def tie(value, after):
    return pl.pallas_call(
        tie_kernel,
        out_shape=jax.ShapeDtypeStruct(value.shape, value.dtype),
        in_specs=[anywhere(), anywhere()],
        out_specs=anywhere(),
        input_output_aliases={0: 0},
        name="tie",
    )(value, after)


def join_kernel(*refs):
    out_ref = refs[-1]
    for n, ref in enumerate(refs[:-1]):
        out_ref[n * 64 : (n + 1) * 64, :] = ref[64:, :]


def join(parts):
    return pl.pallas_call(
        join_kernel,
        out_shape=jax.ShapeDtypeStruct((len(parts) * 64, WIDTH), bf16),
        in_specs=[whole()] * len(parts),
        out_specs=whole(),
        compiler_params=params(),
        cost_estimate=pl.CostEstimate(flops=0, bytes_accessed=2_000_000, transcendentals=0),
        name="join",
    )(*parts)


def level_from(value, away):
    pairs = [
        ((level + away) % LEVELS * 2 + core, level * 2 + core)
        for level in range(LEVELS)
        for core in range(2)
    ]
    return lax.ppermute(value, "ctx", pairs)


def swap(value):
    return lax.ppermute(value, "ctx", [(at, at ^ 1) for at in range(2 * LEVELS)])


def exchange(rows):
    parts = rows.reshape(PLANE, rows.shape[0] // PLANE, rows.shape[1])
    got = lax.all_to_all(parts, "pb", split_axis=0, concat_axis=0, tiled=True)
    return got.reshape(rows.shape)


def outer_levels(chunks):
    groups = [
        [(outer * 4 + inner) * 2 + core for outer in range(4)]
        for inner in range(4)
        for core in range(2)
    ]
    got = lax.all_to_all(
        chunks, "ctx", split_axis=0, concat_axis=0, axis_index_groups=groups, tiled=True
    )
    return got.reshape(chunks.shape[0] * chunks.shape[1], chunks.shape[2])


def local(q_latent, kv_cache, index_queries, index_weights, index_keys, q_blocks):
    kv_turned = kv_cache.T
    z, y = pack(kv_turned, index_keys, index_queries, index_weights, q_blocks)
    held = outer_levels(z)
    y = lax.all_to_all(y, "pb", split_axis=0, concat_axis=0, tiled=True)
    across = swap(held)
    others = [level_from(held, 1), level_from(held, 15), two_levels_on(held)]
    near = exchange(gather("near", NEAR, [held, across], y, others))
    swapped = [swap(other) for other in others]
    tables = [held] + others + [across] + swapped
    scores, asked = score(tables, y)
    sent = gather("far", FAR, others + swapped, y, [], scores)
    served = serve(kv_turned, asked, sent)
    far = exchange(tie(sent, near))
    mine = [served[0]]
    for away in AWAYS[1:]:
        mine.append(level_from(served[AWAYS.index(-away % LEVELS)], away))
    crossed = swap(join(mine))
    query = q_latent.reshape(2, HEADS, DQK)
    before, state, scores = attend_plane(query, q_blocks, near, far)
    return (attend_column(query, q_blocks, before, state, mine, crossed), scores)


def solution(mesh):
    in_specs = (
        P(("ctx", "pb"), None),
        P("ctx", None),
        P(("ctx", "pb"), None),
        P(("ctx", "pb"), None),
        P(("ctx", "pb"), None),
        P(("ctx", "pb"), None),
    )
    out_specs = (P(("ctx", "pb"), None), P(("ctx", "pb"), None))
    return jax.shard_map(local, mesh=mesh, in_specs=in_specs, out_specs=out_specs, check_vma=False)
```

```python
import functools

import jax
import jax.numpy as jnp
from jax import lax
from jax.experimental import pallas as pl
from jax.experimental.pallas import tpu as pltpu
from jax.sharding import PartitionSpec as P

DL = 512
DQK = 576
ROT = DQK - DL
BLK = 64
IH = 64
ID = 128
HEADS = 128
PLANE = 16
LEVELS = 16
PIECE = BLK // PLANE
KV_COLS = PIECE * DQK
WIDTH = KV_COLS // 2
IDS_AT = KV_COLS + 4 * ID
Z_COLS = IDS_AT + 128
SENT_COLS = KV_COLS + 128
AWAYS = (0, 1, 2, 14, 15)
VMEM_LIMIT = 24 * 1024 * 1024

score_scale = 192.0 ** (-0.5)
index_scale = 128.0 ** (-0.5)
f32 = jnp.float32
bf16 = jnp.bfloat16

NEAR = (0, 64, 12)
FAR = (64, 192, 32)


def params(limit=VMEM_LIMIT):
    return pltpu.CompilerParams(vmem_limit_bytes=limit)


def whole():
    return pl.BlockSpec(memory_space=pltpu.VMEM)


def anywhere():
    return pl.BlockSpec(memory_space=pl.ANY)


def main_memory():
    return pl.BlockSpec(memory_space=pltpu.HBM)


def iota(shape, dim):
    return lax.broadcasted_iota(jnp.int32, shape, dim)


def table_row(block):
    at = lax.axis_index("ctx")
    half = (block // 8 + at) % 2
    turn = (block // 16 - at // 2 + LEVELS) % 4
    order = jnp.where(turn == 3, 2, jnp.where(turn == 2, 3, turn))
    inner = block // 64 * 8 + block % 8
    return jnp.where(
        order == 0, half * 32 + inner, 64 + half * 96 + (order - 1) * 32 + inner
    )


def slot_shard(span, t):
    level = lax.axis_index("ctx") // 2
    if span is NEAR:
        away = (t % 32 // 8 * 4 + level % 4 - level + LEVELS) % LEVELS
        return jnp.where(away == 0, -1, t // 32 * 3 + away // 4 - 1)
    order = t % 96 // 32
    step = jnp.where(order == 0, 1, jnp.where(order == 1, 3, 2))
    away = (t % 32 // 8 * 4 + (level + step) % 4 - level + LEVELS) % LEVELS
    which = jnp.where(order == 1, away // 4, away // 4 - 1)
    return jnp.where((away > 2) & (away < 14), t // 96 * 8 + order * 3 + which, -1)


def pack_kernel(*refs):
    sources, (z_ref, y_ref, keys, rows), targets, sem = refs[:5], refs[5:9], refs[9:14], refs[14]
    copies = [
        pltpu.make_async_copy(source, target, sem.at[n])
        for n, (source, target) in enumerate(zip(sources, targets))
    ]
    for copy in copies:
        copy.start()
    for copy in copies:
        copy.wait()
    kv_ref, ik_ref, iq_ref, iw_ref, qb_ref = targets
    piece = lax.axis_index("pb")
    shard_keys = kv_ref.shape[1]
    line = iota((PIECE * 8, shard_keys), 0)
    source = (line % 8) * BLK + piece * PIECE + line // 8
    select = jnp.where(source == iota(source.shape, 1), 1.0, 0.0).astype(bf16)
    part = lax.dot_general(
        select, kv_ref[...], (((1,), (1,)), ((), ())), preferred_element_type=f32
    )
    keys[...] = ik_ref[...].astype(f32)
    ids = qb_ref[...].astype(f32)
    ids = jnp.concatenate([ids[0:1], ids[1:2], jnp.zeros((1, 64), f32)], axis=1)
    columns = []
    for r in range(0, PIECE, 2):
        pair = (part[r * 8 : (r + 1) * 8], part[(r + 1) * 8 : (r + 2) * 8])
        columns += [rows_of[:, :DL] for rows_of in pair] + [rows_of[:, DL:] for rows_of in pair]
    columns += [keys[pl.ds(j, 8, stride=4), :] for j in range(4)]
    columns.append(jnp.where(iota((8, 128), 0) == 0, ids, 0.0))
    chunk = jnp.concatenate(columns, axis=1).astype(bf16)
    for n in range(4):
        z_ref[n] = chunk
    for h in range(IH):
        rows[pl.ds(h, 2, stride=IH), :] = iq_ref[:, h * ID : (h + 1) * ID].astype(f32)
    weights = iw_ref[...].astype(f32)
    weights = jnp.concatenate([weights[0:1], weights[1:2]], axis=1)
    at = iota((16, 128), 0)
    tail = jnp.where(at == 0, weights, jnp.where(at == 1, ids, 0.0)).astype(bf16)
    head = rows[...].astype(bf16)
    for p in range(PLANE):
        y_ref[p, 0 : 2 * IH, :] = head
        y_ref[p, 2 * IH : 2 * IH + 16, :] = tail


def pack(kv_turned, index_keys, index_queries, index_weights, q_blocks):
    return pl.pallas_call(
        pack_kernel,
        out_shape=(
            jax.ShapeDtypeStruct((4, 8, Z_COLS), bf16),
            jax.ShapeDtypeStruct((PLANE, 2 * IH + 16, ID), bf16),
        ),
        in_specs=[main_memory()] * 5,
        out_specs=(whole(), whole()),
        scratch_shapes=[pltpu.VMEM((32, ID), f32), pltpu.VMEM((2 * IH, ID), f32)]
        + [
            pltpu.VMEM(value.shape, value.dtype)
            for value in (kv_turned, index_keys, index_queries, index_weights, q_blocks)
        ]
        + [pltpu.SemaphoreType.DMA((5,))],
        compiler_params=params(60 * 1024 * 1024),
        name="pack",
    )(kv_turned, index_keys, index_queries, index_weights, q_blocks)


def named_columns(span, ids):
    first, count, unused = span
    lane = iota((count, 128), 1)
    named = jnp.zeros((count, 128), f32)
    for n, row in enumerate(ids):
        place = table_row(row) - first
        hit = jnp.where(place == iota((count, row.shape[1]), 0), 1.0, 0.0)
        named = jnp.where(lane == n, jnp.max(hit, axis=1, keepdims=True), named)
    return named


def slot_codes(span, named):
    count = span[1]
    t, u = iota((count, count), 0), iota((count, count), 1)
    before = jnp.where((t // 8 == u // 8) & (u < t), 1.0, 0.0).astype(bf16)
    rank = jnp.dot(before, named.astype(bf16), preferred_element_type=f32)
    return jnp.where(named > 0.5, rank, -1.0)


def slot_keys(span, named):
    code = slot_codes(span, named)
    shard = slot_shard(span, iota((span[1], 1), 0)).astype(f32)
    return jnp.where((code >= 0.0) & (shard >= 0.0), shard * 2.0 + code, -1.0)


def gather_kernel(span, tables, y_ref, scores_ref, out_ref, onehot):
    first, count, slots = span
    rows = [
        y_ref[p, 2 * IH : 2 * IH + 16, :].astype(f32)[1:2, :64].astype(jnp.int32)
        for p in range(PLANE)
    ]
    keys = slot_keys(span, named_columns(span, rows))
    halves = 2 if span is NEAR else 1
    each = halves * slots
    pad = -count % 128
    keys = jnp.concatenate([keys, jnp.zeros((pad, 128), f32)], axis=0)
    keys = jnp.concatenate([keys.T[:PLANE, :count]] * halves, axis=1)
    line, lane = iota((each, halves * count), 0), iota((each, halves * count), 1)
    half = jnp.where(line >= slots, 1, 0)
    there = jnp.where(lane >= count, 1, 0)
    wanted = jnp.where(half == there, line - half * slots, -5).astype(f32)
    picks = [jnp.where(keys[p : p + 1] == wanted, 1.0, 0.0) for p in range(PLANE)]
    onehot[...] = jnp.concatenate(picks, axis=0).astype(bf16)
    columns = KV_COLS // halves
    for c in range(columns // 384):
        rows = [
            ref[:, h * columns + c * 384 : h * columns + (c + 1) * 384]
            for h in range(halves)
            for ref in tables
        ]
        out_ref[:, c * 384 : (c + 1) * 384] = jnp.dot(
            onehot[...], jnp.concatenate(rows, axis=0), preferred_element_type=f32
        ).astype(bf16)
    if scores_ref is not None:
        for p in range(PLANE):
            at = p * each
            out_ref[at : at + 16, columns:] = scores_ref[p]
            out_ref[at + 16 : at + each, columns:] = jnp.zeros((each - 16, 128), bf16)


def gather(name, span, tables, y, afters, scores=None):
    first, count, slots = span

    def body(*refs):
        refs = list(refs)
        held = [refs.pop(0) for table in tables]
        y_ref = refs.pop(0)
        scores_ref = None
        for after in afters:
            refs.pop(0)
        if scores is not None:
            scores_ref = refs.pop(0)
        gather_kernel(span, held, y_ref, scores_ref, *refs)

    halves = 2 if span is NEAR else 1
    operands = [*tables, y, *afters]
    in_specs = [whole()] * (len(tables) + 1) + [anywhere()] * len(afters)
    columns = WIDTH
    if scores is not None:
        operands.append(scores)
        in_specs.append(whole())
        columns = SENT_COLS
    return pl.pallas_call(
        body,
        out_shape=jax.ShapeDtypeStruct((PLANE * halves * slots, columns), bf16),
        in_specs=in_specs,
        out_specs=whole(),
        scratch_shapes=[pltpu.VMEM((PLANE * halves * slots, halves * count), bf16)],
        compiler_params=params(),
        cost_estimate=pl.CostEstimate(
            flops=2 * PLANE * slots * 4 * count * WIDTH,
            bytes_accessed=3_000_000,
            transcendentals=0,
        ),
        name=name,
    )(*operands)


def serve_kernel(kv_ref, ids_ref, after_ref, *outs):
    at = lax.axis_index("ctx")
    ids = ids_ref[:, :64]
    own = (at * 8).astype(f32)
    lane = iota((16, 512), 1)
    codes = jnp.full((16, 512), -1.0, f32)
    taken = jnp.zeros((16, 1), f32)
    for b in range(8):
        hit = jnp.max(jnp.where(ids == own + b, 1.0, 0.0), axis=1, keepdims=True)
        codes = jnp.where((lane // BLK == b) & (hit > 0.5), taken, codes)
        taken = taken + hit
    row, lane = iota((64, 512), 0), iota((64, 512), 1)
    kind = (row // 32).astype(f32)
    for n in range(len(AWAYS)):
        select = jnp.concatenate(
            [
                jnp.where(
                    (row % 32 + 32 * half == lane % BLK) & (codes[m : m + 1, :] == kind),
                    1.0,
                    0.0,
                )
                for half in range(2)
                for m in (2 * n, 2 * n + 1)
            ],
            axis=0,
        ).astype(bf16)
        got = lax.dot_general(
            select, kv_ref[...], (((1,), (1,)), ((), ())), preferred_element_type=f32
        )
        got = (got[:128], got[128:])
        columns = [part[:, :DL] for part in got] + [part[:, DL:] for part in got]
        outs[n][...] = jnp.concatenate(columns, axis=1).astype(bf16)


def serve(kv_turned, ids, after):
    return pl.pallas_call(
        serve_kernel,
        out_shape=tuple(jax.ShapeDtypeStruct((2 * BLK, WIDTH), bf16) for away in AWAYS),
        in_specs=[whole()] * 2 + [anywhere()],
        out_specs=(whole(),) * len(AWAYS),
        compiler_params=params(),
        cost_estimate=pl.CostEstimate(
            flops=2 * 10 * 128 * 512 * DQK, bytes_accessed=4_000_000, transcendentals=0
        ),
        name="serve",
    )(kv_turned, ids, after)


def score_kernel(*refs):
    tables, (y_ref, out_ref, ids_ref, keys) = refs[:8], refs[8:]
    tail = jnp.concatenate(
        [y_ref[p, 2 * IH : 2 * IH + 16, :].astype(f32)[0:1] for p in range(PLANE)], axis=0
    )
    weights = jnp.concatenate(
        [tail * index_scale, jnp.zeros((128 - PLANE, 128), f32)], axis=0
    ).T
    at = lax.axis_index("ctx")
    level = at // 2
    lines = []
    line = iota((32, 128), 0)
    for away in AWAYS:
        outer = (level + away) % LEVELS // 4
        for other in range(2):
            ref = tables[(0, 1, 3, 2)[away % 4] + 4 * other]
            values = jnp.where(line == outer * 8, ref[:, IDS_AT:].astype(f32), 0.0)
            lines.append(jnp.sum(values, axis=0, keepdims=True))
    lines += [jnp.full((6, 128), -1.0, f32)]
    ids_ref[...] = jnp.concatenate(lines, axis=0)
    lane = iota((128, 128), 1)
    for n, ref in enumerate(tables):
        step = (0, 1, 3, 2)[n % 4]
        inner = (at // 2 + step) % 4
        core = (at + n // 4) % 2
        for outer in range(4):
            shard = (outer * 4 + inner) * 2 + core
            for j in range(4):
                cols = slice(KV_COLS + j * ID, KV_COLS + (j + 1) * ID)
                keys[pl.ds(shard * 32 + j, 8, stride=4), :] = ref[
                    outer * 8 : (outer + 1) * 8, cols
                ].astype(f32)
    key_rows = keys[...].astype(bf16)

    def peers(g, carry):
        products = lax.dot_general(
            y_ref[pl.ds(g * 4, 4), 0 : 2 * IH, :].reshape(8 * IH, ID),
            key_rows,
            (((1,), (1,)), ((), ())),
            preferred_element_type=f32,
        )
        for m in range(4):
            weight = jnp.sum(
                jnp.where(lane == g * 4 + m, weights, 0.0), axis=1, keepdims=True
            )
            active = jnp.maximum(products[m * 2 * IH : (m + 1) * 2 * IH], 0.0) * weight
            lines = []
            for i in range(2):
                total = jnp.sum(active[i * IH : (i + 1) * IH], axis=0, keepdims=True)
                lines += [total[:, c * 128 : (c + 1) * 128] for c in range(8)]
            out_ref[g * 4 + m] = jnp.concatenate(lines, axis=0).astype(bf16)
        return carry

    lax.fori_loop(0, PLANE // 4, peers, 0)


def score(tables, y):
    return pl.pallas_call(
        score_kernel,
        out_shape=(
            jax.ShapeDtypeStruct((PLANE, 16, 128), bf16),
            jax.ShapeDtypeStruct((16, 128), f32),
        ),
        in_specs=[whole()] * 9,
        out_specs=(whole(), whole()),
        scratch_shapes=[pltpu.VMEM((1024, ID), f32)],
        compiler_params=params(),
        cost_estimate=pl.CostEstimate(
            flops=2 * 2048 * 128 * 1024, bytes_accessed=2_000_000, transcendentals=0
        ),
        name="score",
    )(*tables, y)


def product(left, right):
    return lax.dot_general(
        left, right, (((1,), (1,)), ((), ())), preferred_element_type=f32
    )


def attend_start(q_ref, scores):
    ctx = lax.axis_index("ctx")
    rank = ctx * PLANE + lax.axis_index("pb")
    own_block = 240 + rank * 2 // BLK
    offsets = [((rank * 2 + i) % BLK).astype(f32) for i in range(2)]
    query = jnp.concatenate([q_ref[0], q_ref[1]], axis=0)
    latent, rotary = query[:, :DL], query[:, DL:]
    nothing = jnp.zeros_like(rotary)
    padded = (
        jnp.concatenate([latent, rotary, nothing], axis=1),
        jnp.concatenate([latent, nothing, rotary], axis=1),
    )
    sets = []
    filled = [0]
    tops = [jnp.full((HEADS, 128), -1e30, f32) for i in range(2)]

    def keep(block, place, limits, values):
        at, width = filled[0], block.shape[1]
        for i in range(2):
            heads = slice(i * HEADS, (i + 1) * HEADS)
            value = jnp.where(place < limits[i], block[heads], -1e30)
            scores[heads, at : at + width] = value
            for k in range(0, width, 128):
                tops[i] = jnp.maximum(tops[i], value[:, k : k + 128])
        sets.append((at, width, values))
        filled[0] += width

    return ctx, own_block, offsets, padded, sets, tops, keep


def attend_sum(scores, sets, highest, norm, total, fresh):
    for at, width, values in sets:
        weight = jnp.exp((scores[:, at : at + width] - highest) * score_scale)
        for k in range(0, width, 128):
            norm = norm + weight[:, k : k + 128]
        rows = [ref[rows, columns] for ref, rows, columns in values]
        rows = rows[0] if len(rows) == 1 else jnp.concatenate(rows, axis=0)
        term = jnp.dot(weight.astype(bf16), rows, preferred_element_type=f32)
        for k in range(4):
            if fresh:
                total[k] = term[:, k * 128 : (k + 1) * 128]
            else:
                total[k] += term[:, k * 128 : (k + 1) * 128]
        fresh = False
    return norm


def plane_kernel(span, q_ref, ids_ref, ref, *refs):
    if span is NEAR:
        after_ref, total, state, scores = refs
    else:
        before, was, total, state, index_ref, scores, turned = refs
        far_ref = ref
    ctx, own_block, offsets, padded, sets, tops, keep = attend_start(q_ref, scores)
    ids = ids_ref[...]
    own_row = table_row(own_block)
    step = 384 if span is NEAR else 256
    first, count, slots = span
    one, two = named_columns(span, [ids[0:1]]), named_columns(span, [ids[1:2]])
    members = (one[:, 0:1], two[:, 0:1])
    keys = slot_keys(span, jnp.maximum(one, two))[:, 0:1]
    halves = 2 if span is NEAR else 1
    width = PLANE * halves * slots
    line = iota((count, 128), 0)
    chosen = keys == (iota((1, width), 1) % slots).astype(f32)
    limits = []
    for i in range(2):
        limit = jnp.where(line[:, 0:1] + first == own_row, offsets[i], 63.0) + 1.0
        limit = jnp.where(members[i] > 0.5, limit, 0.0)
        limits.append(jnp.sum(jnp.where(chosen, limit, 0.0), axis=0, keepdims=True))
    lane = iota((1, width), 1)
    place = lane // (halves * slots) * PIECE
    if halves == 2:
        place = place + lane // slots % 2 * 2
    for k in range(width // step):
        rows = slice(k * step, (k + 1) * step)
        for r in range(PIECE // halves):
            half, parity = r // 2, r % 2
            at = half * WIDTH + parity * DL
            columns = slice(at, at + DL)
            turn = half * WIDTH + 2 * DL
            block = product(
                padded[parity],
                jnp.concatenate([ref[rows, columns], ref[rows, turn : turn + 128]], axis=1),
            )
            keep(
                block,
                (place[:, rows] + r).astype(f32),
                [limit[:, rows] for limit in limits],
                [(ref, rows, columns)],
            )

    highest = jnp.max(jnp.concatenate(tops, axis=0), axis=1, keepdims=True)
    if span is NEAR:
        norm = jnp.zeros((2 * HEADS, 128), f32)
        state[0] = jnp.broadcast_to(highest, (2 * HEADS, 128))
        state[1] = attend_sum(scores, sets, highest, norm, total, True)
        return
    highest = jnp.maximum(highest, was[0][:, 0:1])
    fade = jnp.exp((was[0] - highest) * score_scale)
    for k in range(4):
        total[k] = before[k] * fade
    state[0] = jnp.broadcast_to(highest, (2 * HEADS, 128))
    state[1] = attend_sum(scores, sets, highest, was[1] * fade, total, False)

    tiles = [
        far_ref[p * FAR[2] : p * FAR[2] + 16, KV_COLS:].astype(f32)
        for p in range(PLANE)
    ]
    group = iota((16, 128), 1) // 32
    for c in range(4):
        for m in range(4):
            mixed = tiles[4 * m]
            for k in range(4):
                tile = tiles[4 * m + k]
                if k != c:
                    tile = pltpu.roll(tile, (k - c) * 32 % 128, 1)
                mixed = tile if k == 0 else jnp.where(group == k, tile, mixed)
            turned[(c * 4 + m) * 16 : (c * 4 + m + 1) * 16, :] = mixed
            for t in range(8):
                at = (t * 4 + c) * 512 + m * 128
                index_ref[:, at : at + 128] = turned[
                    pl.ds((c * 4 + m) * 16 + t, 2, stride=8), :
                ].astype(bf16)


def column_kernel(q_ref, ids_ref, before, state, *refs):
    count = len(AWAYS)
    mine, crossed, (out_ref, scores, total) = refs[:count], refs[count], refs[count + 1 :]
    ctx, own_block, offsets, padded, sets, tops, keep = attend_start(q_ref, scores)
    ids = ids_ref[...]
    count = 16 * len(AWAYS)
    line = iota((count, 128), 0)
    lane = iota((count, 128), 1)
    named = jnp.zeros((count, 128), f32)
    shard = ids // 8
    away = (shard // 2 - ctx // 2 + LEVELS) % LEVELS
    turn = jnp.where(away < 3, away, jnp.where(away > 13, away - 11, -8))
    place = (turn * 2 + (shard + ctx) % 2) * 8 + ids % 8
    own_away = (own_block // 16 - ctx // 2 + LEVELS) % LEVELS
    own_turn = jnp.where(own_away < 3, own_away, jnp.where(own_away > 13, own_away - 11, -8))
    own_place = (own_turn * 2 + (own_block // 8 + ctx) % 2) * 8 + own_block % 8
    for i in range(2):
        hit = jnp.where(place[i : i + 1] == iota((count, ids.shape[1]), 0), 1.0, 0.0)
        named = jnp.where(lane == i, jnp.max(hit, axis=1, keepdims=True), named)
    members = named
    named = jnp.maximum(named[:, 0:1], named[:, 1:2])
    code = slot_codes((0, count, 2), jnp.broadcast_to(named, (count, 128)))
    chosen = code == (lane // 32 % 2).astype(f32)
    limits = []
    for i in range(2):
        limit = jnp.where(line[:, 0:1] == own_place, offsets[i], 63.0) + 1.0
        limit = jnp.where(members[:, i : i + 1] > 0.5, limit, 0.0)
        limits.append(jnp.where(chosen, limit, 0.0))
    low = iota((1, 128), 1) < 64
    shown = [
        [
            jnp.where(
                low,
                jnp.sum(limit[n * 8 : (n + 1) * 8], axis=0, keepdims=True),
                jnp.sum(limit[(n + 1) * 8 : (n + 2) * 8], axis=0, keepdims=True),
            )
            for n in range(0, 2 * len(AWAYS), 2)
        ]
        for limit in limits
    ]
    here = iota((1, 128), 1) % 32
    direct = []
    for n in range(len(AWAYS)):
        direct += [(mine[n], slice(0, 64)), (crossed, slice(n * 64, (n + 1) * 64))]
    for first, last in ((0, 2), (2, 4), (4, 5)):
        parts = direct[2 * first : 2 * last]
        turns = [ref[rows, 2 * DL : 2 * DL + 128] for ref, rows in parts]
        for parity in range(2):
            columns = slice(parity * DL, (parity + 1) * DL)
            values = [ref[rows, columns] for ref, rows in parts]
            both = [jnp.concatenate(pair, axis=1) for pair in zip(values, turns)]
            keep(
                product(padded[parity], jnp.concatenate(both, axis=0)),
                jnp.concatenate([(here + 32 * parity).astype(f32)] * (last - first), axis=1),
                [jnp.concatenate(each[first:last], axis=1) for each in shown],
                [(ref, rows, columns) for ref, rows in parts],
            )

    highest = jnp.max(jnp.concatenate(tops, axis=0), axis=1, keepdims=True)
    highest = jnp.maximum(highest, state[0][:, 0:1])
    fade = jnp.exp((state[0] - highest) * score_scale)
    for k in range(4):
        total[k] = before[k] * fade
    norm = attend_sum(scores, sets, highest, state[1] * fade, total, False)
    share = 1.0 / jnp.sum(norm, axis=1, keepdims=True)
    for k in range(4):
        total[k] = total[k] * share
    for h in range(HEADS):
        for k in range(4):
            at = h * DL + k * 128
            out_ref[:, at : at + 128] = total[k, pl.ds(h, 2, stride=HEADS), :].astype(bf16)


STATES = (
    jax.ShapeDtypeStruct((4, 2 * HEADS, 128), f32),
    jax.ShapeDtypeStruct((2, 2 * HEADS, 128), f32),
)


def attend_near(query, ids, near, after):
    return pl.pallas_call(
        functools.partial(plane_kernel, NEAR),
        out_shape=STATES,
        in_specs=[whole()] * 3 + [anywhere()],
        out_specs=(whole(),) * 2,
        scratch_shapes=[pltpu.VMEM((2 * HEADS, 768), f32)],
        compiler_params=params(),
        cost_estimate=pl.CostEstimate(
            flops=2 * 256 * 768 * 1152, bytes_accessed=2_000_000, transcendentals=256 * 768
        ),
        name="attend_near",
    )(query, ids, near, after)


def attend_far(query, ids, far, before, state):
    return pl.pallas_call(
        functools.partial(plane_kernel, FAR),
        out_shape=STATES + (jax.ShapeDtypeStruct((2, 16384), bf16),),
        in_specs=[whole()] * 5,
        out_specs=(whole(),) * 3,
        scratch_shapes=[
            pltpu.VMEM((2 * HEADS, 2048), f32),
            pltpu.VMEM((256, 128), f32),
        ],
        compiler_params=params(),
        cost_estimate=pl.CostEstimate(
            flops=2 * 256 * 2048 * 1152, bytes_accessed=4_000_000, transcendentals=256 * 2048
        ),
        name="attend_far",
    )(query, ids, far, before, state)


def attend_column(query, ids, before, state, mine, crossed):
    return pl.pallas_call(
        column_kernel,
        out_shape=jax.ShapeDtypeStruct((2, HEADS * DL), bf16),
        in_specs=[whole()] * (5 + len(mine)),
        out_specs=whole(),
        scratch_shapes=[
            pltpu.VMEM((2 * HEADS, 1280), f32),
            pltpu.VMEM((4, 2 * HEADS, 128), f32),
        ],
        compiler_params=params(),
        cost_estimate=pl.CostEstimate(
            flops=2 * 256 * 1280 * 1152, bytes_accessed=3_000_000, transcendentals=256 * 1280
        ),
        name="attend_column",
    )(query, ids, before, state, *mine, crossed)


def two_levels_on(value):
    pairs = [
        ((level + (2, -2)[core]) % LEVELS * 2 + core, level * 2 + core)
        for level in range(LEVELS)
        for core in range(2)
    ]
    return lax.ppermute(value, "ctx", pairs)


def tie_kernel(value_ref, after_ref, out_ref):
    pass


def tie(value, after):
    return pl.pallas_call(
        tie_kernel,
        out_shape=jax.ShapeDtypeStruct(value.shape, value.dtype),
        in_specs=[anywhere(), anywhere()],
        out_specs=anywhere(),
        input_output_aliases={0: 0},
        name="tie",
    )(value, after)


def join_kernel(*refs):
    out_ref = refs[-1]
    for n, ref in enumerate(refs[:-1]):
        out_ref[n * 64 : (n + 1) * 64, :] = ref[64:, :]


def join(parts):
    return pl.pallas_call(
        join_kernel,
        out_shape=jax.ShapeDtypeStruct((len(parts) * 64, WIDTH), bf16),
        in_specs=[whole()] * len(parts),
        out_specs=whole(),
        compiler_params=params(),
        cost_estimate=pl.CostEstimate(flops=0, bytes_accessed=2_000_000, transcendentals=0),
        name="join",
    )(*parts)


def level_from(value, away):
    pairs = [
        ((level + away) % LEVELS * 2 + core, level * 2 + core)
        for level in range(LEVELS)
        for core in range(2)
    ]
    return lax.ppermute(value, "ctx", pairs)


def swap(value):
    return lax.ppermute(value, "ctx", [(at, at ^ 1) for at in range(2 * LEVELS)])


def exchange(rows):
    parts = rows.reshape(PLANE, rows.shape[0] // PLANE, rows.shape[1])
    got = lax.all_to_all(parts, "pb", split_axis=0, concat_axis=0, tiled=True)
    return got.reshape(rows.shape)


def outer_levels(chunks):
    groups = [
        [(outer * 4 + inner) * 2 + core for outer in range(4)]
        for inner in range(4)
        for core in range(2)
    ]
    got = lax.all_to_all(
        chunks, "ctx", split_axis=0, concat_axis=0, axis_index_groups=groups, tiled=True
    )
    return got.reshape(chunks.shape[0] * chunks.shape[1], chunks.shape[2])


def local(q_latent, kv_cache, index_queries, index_weights, index_keys, q_blocks):
    kv_turned = kv_cache.T
    z, y = pack(kv_turned, index_keys, index_queries, index_weights, q_blocks)
    held = outer_levels(z)
    y = lax.all_to_all(y, "pb", split_axis=0, concat_axis=0, tiled=True)
    across = swap(held)
    others = [level_from(held, 1), level_from(held, 15), two_levels_on(held)]
    near = exchange(gather("near", NEAR, [held, across], y, others))
    swapped = [swap(other) for other in others]
    tables = [held] + others + [across] + swapped
    scores, asked = score(tables, y)
    sent = gather("far", FAR, others + swapped, y, [], scores)
    served = serve(kv_turned, asked, sent)
    far = exchange(tie(sent, near))
    mine = [served[0]]
    for away in AWAYS[1:]:
        mine.append(level_from(served[AWAYS.index(-away % LEVELS)], away))
    crossed = swap(join(mine))
    query = q_latent.reshape(2, HEADS, DQK)
    before, state = attend_near(query, q_blocks, near, mine[1])
    before, state, scores = attend_far(query, q_blocks, far, before, state)
    return (attend_column(query, q_blocks, before, state, mine, crossed), scores)


def solution(mesh):
    in_specs = (
        P(("ctx", "pb"), None),
        P("ctx", None),
        P(("ctx", "pb"), None),
        P(("ctx", "pb"), None),
        P(("ctx", "pb"), None),
        P(("ctx", "pb"), None),
    )
    out_specs = (P(("ctx", "pb"), None), P(("ctx", "pb"), None))
    return jax.shard_map(local, mesh=mesh, in_specs=in_specs, out_specs=out_specs, check_vma=False)
```

```python
import jax
import jax.numpy as jnp
from jax import lax
from jax.experimental import pallas as pl
from jax.experimental.pallas import tpu as pltpu
from jax.sharding import PartitionSpec as P

DL = 512
DQK = 576
ROT = DQK - DL
BLK = 64
IH = 64
ID = 128
HEADS = 128
PLANE = 16
LEVELS = 16
PIECE = BLK // PLANE
KV_COLS = PIECE * DQK
WIDTH = KV_COLS // 2
IDS_AT = KV_COLS + 4 * ID
Z_COLS = IDS_AT + 128
SENT_COLS = KV_COLS + 128
AWAYS = (0, 1, 2, 14, 15)
VMEM_LIMIT = 24 * 1024 * 1024

score_scale = 192.0 ** (-0.5)
index_scale = 128.0 ** (-0.5)
f32 = jnp.float32
bf16 = jnp.bfloat16

NEAR = (0, 64, 12)
FAR = (64, 192, 32)


def params(limit=VMEM_LIMIT):
    return pltpu.CompilerParams(vmem_limit_bytes=limit)


def whole():
    return pl.BlockSpec(memory_space=pltpu.VMEM)


def anywhere():
    return pl.BlockSpec(memory_space=pl.ANY)


def main_memory():
    return pl.BlockSpec(memory_space=pltpu.HBM)


def iota(shape, dim):
    return lax.broadcasted_iota(jnp.int32, shape, dim)


def table_row(block):
    at = lax.axis_index("ctx")
    half = (block // 8 + at) % 2
    turn = (block // 16 - at // 2 + LEVELS) % 4
    order = jnp.where(turn == 3, 2, jnp.where(turn == 2, 3, turn))
    inner = block // 64 * 8 + block % 8
    return jnp.where(
        order == 0, half * 32 + inner, 64 + half * 96 + (order - 1) * 32 + inner
    )


def slot_shard(span, t):
    level = lax.axis_index("ctx") // 2
    if span is NEAR:
        away = (t % 32 // 8 * 4 + level % 4 - level + LEVELS) % LEVELS
        return jnp.where(away == 0, -1, t // 32 * 3 + away // 4 - 1)
    order = t % 96 // 32
    step = jnp.where(order == 0, 1, jnp.where(order == 1, 3, 2))
    away = (t % 32 // 8 * 4 + (level + step) % 4 - level + LEVELS) % LEVELS
    which = jnp.where(order == 1, away // 4, away // 4 - 1)
    return jnp.where((away > 2) & (away < 14), t // 96 * 8 + order * 3 + which, -1)


def pack_kernel(*refs):
    sources, (z_ref, y_ref, keys, rows), targets, sem = refs[:5], refs[5:9], refs[9:14], refs[14]
    copies = [
        pltpu.make_async_copy(source, target, sem.at[n])
        for n, (source, target) in enumerate(zip(sources, targets))
    ]
    for copy in copies:
        copy.start()
    for copy in copies:
        copy.wait()
    kv_ref, ik_ref, iq_ref, iw_ref, qb_ref = targets
    piece = lax.axis_index("pb")
    shard_keys = kv_ref.shape[1]
    line = iota((PIECE * 8, shard_keys), 0)
    source = (line % 8) * BLK + piece * PIECE + line // 8
    select = jnp.where(source == iota(source.shape, 1), 1.0, 0.0).astype(bf16)
    part = lax.dot_general(
        select, kv_ref[...], (((1,), (1,)), ((), ())), preferred_element_type=f32
    )
    keys[...] = ik_ref[...].astype(f32)
    ids = qb_ref[...].astype(f32)
    ids = jnp.concatenate([ids[0:1], ids[1:2], jnp.zeros((1, 64), f32)], axis=1)
    columns = []
    for r in range(0, PIECE, 2):
        pair = (part[r * 8 : (r + 1) * 8], part[(r + 1) * 8 : (r + 2) * 8])
        columns += [rows_of[:, :DL] for rows_of in pair] + [rows_of[:, DL:] for rows_of in pair]
    columns += [keys[pl.ds(j, 8, stride=4), :] for j in range(4)]
    columns.append(jnp.where(iota((8, 128), 0) == 0, ids, 0.0))
    chunk = jnp.concatenate(columns, axis=1).astype(bf16)
    for n in range(4):
        z_ref[n] = chunk
    for h in range(IH):
        rows[pl.ds(h, 2, stride=IH), :] = iq_ref[:, h * ID : (h + 1) * ID].astype(f32)
    weights = iw_ref[...].astype(f32)
    weights = jnp.concatenate([weights[0:1], weights[1:2]], axis=1)
    at = iota((16, 128), 0)
    tail = jnp.where(at == 0, weights, jnp.where(at == 1, ids, 0.0)).astype(bf16)
    head = rows[...].astype(bf16)
    for p in range(PLANE):
        y_ref[p, 0 : 2 * IH, :] = head
        y_ref[p, 2 * IH : 2 * IH + 16, :] = tail


def pack(kv_turned, index_keys, index_queries, index_weights, q_blocks):
    return pl.pallas_call(
        pack_kernel,
        out_shape=(
            jax.ShapeDtypeStruct((4, 8, Z_COLS), bf16),
            jax.ShapeDtypeStruct((PLANE, 2 * IH + 16, ID), bf16),
        ),
        in_specs=[main_memory()] * 5,
        out_specs=(whole(), whole()),
        scratch_shapes=[pltpu.VMEM((32, ID), f32), pltpu.VMEM((2 * IH, ID), f32)]
        + [
            pltpu.VMEM(value.shape, value.dtype)
            for value in (kv_turned, index_keys, index_queries, index_weights, q_blocks)
        ]
        + [pltpu.SemaphoreType.DMA((5,))],
        compiler_params=params(60 * 1024 * 1024),
        name="pack",
    )(kv_turned, index_keys, index_queries, index_weights, q_blocks)


def named_columns(span, ids):
    first, count, unused = span
    lane = iota((count, 128), 1)
    named = jnp.zeros((count, 128), f32)
    for n, row in enumerate(ids):
        place = table_row(row) - first
        hit = jnp.where(place == iota((count, row.shape[1]), 0), 1.0, 0.0)
        named = jnp.where(lane == n, jnp.max(hit, axis=1, keepdims=True), named)
    return named


def slot_codes(span, named):
    count = span[1]
    t, u = iota((count, count), 0), iota((count, count), 1)
    before = jnp.where((t // 8 == u // 8) & (u < t), 1.0, 0.0).astype(bf16)
    rank = jnp.dot(before, named.astype(bf16), preferred_element_type=f32)
    return jnp.where(named > 0.5, rank, -1.0)


def slot_keys(span, named):
    code = slot_codes(span, named)
    shard = slot_shard(span, iota((span[1], 1), 0)).astype(f32)
    return jnp.where((code >= 0.0) & (shard >= 0.0), shard * 2.0 + code, -1.0)


def gather_kernel(span, tables, y_ref, scores_ref, out_ref, onehot):
    first, count, slots = span
    rows = [
        y_ref[p, 2 * IH : 2 * IH + 16, :].astype(f32)[1:2, :64].astype(jnp.int32)
        for p in range(PLANE)
    ]
    keys = slot_keys(span, named_columns(span, rows))
    halves = 2 if span is NEAR else 1
    each = halves * slots
    pad = -count % 128
    keys = jnp.concatenate([keys, jnp.zeros((pad, 128), f32)], axis=0)
    keys = jnp.concatenate([keys.T[:PLANE, :count]] * halves, axis=1)
    line, lane = iota((each, halves * count), 0), iota((each, halves * count), 1)
    half = jnp.where(line >= slots, 1, 0)
    there = jnp.where(lane >= count, 1, 0)
    wanted = jnp.where(half == there, line - half * slots, -5).astype(f32)
    picks = [jnp.where(keys[p : p + 1] == wanted, 1.0, 0.0) for p in range(PLANE)]
    onehot[...] = jnp.concatenate(picks, axis=0).astype(bf16)
    columns = KV_COLS // halves
    for c in range(columns // 384):
        rows = [
            ref[:, h * columns + c * 384 : h * columns + (c + 1) * 384]
            for h in range(halves)
            for ref in tables
        ]
        out_ref[:, c * 384 : (c + 1) * 384] = jnp.dot(
            onehot[...], jnp.concatenate(rows, axis=0), preferred_element_type=f32
        ).astype(bf16)
    if scores_ref is not None:
        for p in range(PLANE):
            at = p * each
            out_ref[at : at + 16, columns:] = scores_ref[p]
            out_ref[at + 16 : at + each, columns:] = jnp.zeros((each - 16, 128), bf16)


def gather(name, span, tables, y, afters, scores=None):
    first, count, slots = span

    def body(*refs):
        refs = list(refs)
        held = [refs.pop(0) for table in tables]
        y_ref = refs.pop(0)
        scores_ref = None
        for after in afters:
            refs.pop(0)
        if scores is not None:
            scores_ref = refs.pop(0)
        gather_kernel(span, held, y_ref, scores_ref, *refs)

    halves = 2 if span is NEAR else 1
    operands = [*tables, y, *afters]
    in_specs = [whole()] * (len(tables) + 1) + [anywhere()] * len(afters)
    columns = WIDTH
    if scores is not None:
        operands.append(scores)
        in_specs.append(whole())
        columns = SENT_COLS
    return pl.pallas_call(
        body,
        out_shape=jax.ShapeDtypeStruct((PLANE * halves * slots, columns), bf16),
        in_specs=in_specs,
        out_specs=whole(),
        scratch_shapes=[pltpu.VMEM((PLANE * halves * slots, halves * count), bf16)],
        compiler_params=params(),
        cost_estimate=pl.CostEstimate(
            flops=2 * PLANE * slots * 4 * count * WIDTH,
            bytes_accessed=3_000_000,
            transcendentals=0,
        ),
        name=name,
    )(*operands)


def serve_kernel(kv_ref, ids_ref, after_ref, *outs):
    at = lax.axis_index("ctx")
    ids = ids_ref[:, :64]
    own = (at * 8).astype(f32)
    lane = iota((16, 512), 1)
    codes = jnp.full((16, 512), -1.0, f32)
    taken = jnp.zeros((16, 1), f32)
    for b in range(8):
        hit = jnp.max(jnp.where(ids == own + b, 1.0, 0.0), axis=1, keepdims=True)
        codes = jnp.where((lane // BLK == b) & (hit > 0.5), taken, codes)
        taken = taken + hit
    row, lane = iota((64, 512), 0), iota((64, 512), 1)
    kind = (row // 32).astype(f32)
    for n in range(len(AWAYS)):
        select = jnp.concatenate(
            [
                jnp.where(
                    (row % 32 + 32 * half == lane % BLK) & (codes[m : m + 1, :] == kind),
                    1.0,
                    0.0,
                )
                for half in range(2)
                for m in (2 * n, 2 * n + 1)
            ],
            axis=0,
        ).astype(bf16)
        got = lax.dot_general(
            select, kv_ref[...], (((1,), (1,)), ((), ())), preferred_element_type=f32
        )
        got = (got[:128], got[128:])
        columns = [part[:, :DL] for part in got] + [part[:, DL:] for part in got]
        outs[n][...] = jnp.concatenate(columns, axis=1).astype(bf16)


def serve(kv_turned, ids, after):
    return pl.pallas_call(
        serve_kernel,
        out_shape=tuple(jax.ShapeDtypeStruct((2 * BLK, WIDTH), bf16) for away in AWAYS),
        in_specs=[whole()] * 2 + [anywhere()],
        out_specs=(whole(),) * len(AWAYS),
        compiler_params=params(),
        cost_estimate=pl.CostEstimate(
            flops=2 * 10 * 128 * 512 * DQK, bytes_accessed=4_000_000, transcendentals=0
        ),
        name="serve",
    )(kv_turned, ids, after)


def score_kernel(*refs):
    tables, (y_ref, out_ref, ids_ref, keys) = refs[:8], refs[8:]
    tail = jnp.concatenate(
        [y_ref[p, 2 * IH : 2 * IH + 16, :].astype(f32)[0:1] for p in range(PLANE)], axis=0
    )
    weights = jnp.concatenate(
        [tail * index_scale, jnp.zeros((128 - PLANE, 128), f32)], axis=0
    ).T
    at = lax.axis_index("ctx")
    level = at // 2
    lines = []
    line = iota((32, 128), 0)
    for away in AWAYS:
        outer = (level + away) % LEVELS // 4
        for other in range(2):
            ref = tables[(0, 1, 3, 2)[away % 4] + 4 * other]
            values = jnp.where(line == outer * 8, ref[:, IDS_AT:].astype(f32), 0.0)
            lines.append(jnp.sum(values, axis=0, keepdims=True))
    lines += [jnp.full((6, 128), -1.0, f32)]
    ids_ref[...] = jnp.concatenate(lines, axis=0)
    lane = iota((128, 128), 1)
    for n, ref in enumerate(tables):
        step = (0, 1, 3, 2)[n % 4]
        inner = (at // 2 + step) % 4
        core = (at + n // 4) % 2
        for outer in range(4):
            shard = (outer * 4 + inner) * 2 + core
            for j in range(4):
                cols = slice(KV_COLS + j * ID, KV_COLS + (j + 1) * ID)
                keys[pl.ds(shard * 32 + j, 8, stride=4), :] = ref[
                    outer * 8 : (outer + 1) * 8, cols
                ].astype(f32)
    key_rows = keys[...].astype(bf16)

    def peers(g, carry):
        products = lax.dot_general(
            y_ref[pl.ds(g * 4, 4), 0 : 2 * IH, :].reshape(8 * IH, ID),
            key_rows,
            (((1,), (1,)), ((), ())),
            preferred_element_type=f32,
        )
        for m in range(4):
            weight = jnp.sum(
                jnp.where(lane == g * 4 + m, weights, 0.0), axis=1, keepdims=True
            )
            active = jnp.maximum(products[m * 2 * IH : (m + 1) * 2 * IH], 0.0) * weight
            lines = []
            for i in range(2):
                total = jnp.sum(active[i * IH : (i + 1) * IH], axis=0, keepdims=True)
                lines += [total[:, c * 128 : (c + 1) * 128] for c in range(8)]
            out_ref[g * 4 + m] = jnp.concatenate(lines, axis=0).astype(bf16)
        return carry

    lax.fori_loop(0, PLANE // 4, peers, 0)


def score(tables, y):
    return pl.pallas_call(
        score_kernel,
        out_shape=(
            jax.ShapeDtypeStruct((PLANE, 16, 128), bf16),
            jax.ShapeDtypeStruct((16, 128), f32),
        ),
        in_specs=[whole()] * 9,
        out_specs=(whole(), whole()),
        scratch_shapes=[pltpu.VMEM((1024, ID), f32)],
        compiler_params=params(),
        cost_estimate=pl.CostEstimate(
            flops=2 * 2048 * 128 * 1024, bytes_accessed=2_000_000, transcendentals=0
        ),
        name="score",
    )(*tables, y)


def product(left, right):
    return lax.dot_general(
        left, right, (((1,), (1,)), ((), ())), preferred_element_type=f32
    )


def attend_start(q_ref, scores):
    ctx = lax.axis_index("ctx")
    rank = ctx * PLANE + lax.axis_index("pb")
    own_block = 240 + rank * 2 // BLK
    offsets = [((rank * 2 + i) % BLK).astype(f32) for i in range(2)]
    query = jnp.concatenate([q_ref[0], q_ref[1]], axis=0)
    latent, rotary = query[:, :DL], query[:, DL:]
    nothing = jnp.zeros_like(rotary)
    padded = (
        jnp.concatenate([latent, rotary, nothing], axis=1),
        jnp.concatenate([latent, nothing, rotary], axis=1),
    )
    sets = []
    filled = [0]
    tops = [jnp.full((HEADS, 128), -1e30, f32) for i in range(2)]

    def keep(block, place, limits, values):
        at, width = filled[0], block.shape[1]
        for i in range(2):
            heads = slice(i * HEADS, (i + 1) * HEADS)
            value = jnp.where(place < limits[i], block[heads], -1e30)
            scores[heads, at : at + width] = value
            for k in range(0, width, 128):
                tops[i] = jnp.maximum(tops[i], value[:, k : k + 128])
        sets.append((at, width, values))
        filled[0] += width

    return ctx, own_block, offsets, padded, sets, tops, keep


def attend_sum(scores, sets, highest, norm, total, fresh):
    for at, width, values in sets:
        weight = jnp.exp((scores[:, at : at + width] - highest) * score_scale)
        for k in range(0, width, 128):
            norm = norm + weight[:, k : k + 128]
        rows = [ref[rows, columns] for ref, rows, columns in values]
        rows = rows[0] if len(rows) == 1 else jnp.concatenate(rows, axis=0)
        term = jnp.dot(weight.astype(bf16), rows, preferred_element_type=f32)
        for k in range(4):
            if fresh:
                total[k] = term[:, k * 128 : (k + 1) * 128]
            else:
                total[k] += term[:, k * 128 : (k + 1) * 128]
        fresh = False
    return norm


def plane_kernel(q_ref, ids_ref, near_ref, far_ref, total, state, index_ref, scores, turned):
    ctx, own_block, offsets, padded, sets, tops, keep = attend_start(q_ref, scores)
    ids = ids_ref[...]
    own_row = table_row(own_block)
    for span, ref, step in ((NEAR, near_ref, 384), (FAR, far_ref, 512)):
        first, count, slots = span
        one, two = named_columns(span, [ids[0:1]]), named_columns(span, [ids[1:2]])
        members = (one[:, 0:1], two[:, 0:1])
        keys = slot_keys(span, jnp.maximum(one, two))[:, 0:1]
        halves = 2 if span is NEAR else 1
        width = PLANE * halves * slots
        line = iota((count, 128), 0)
        chosen = keys == (iota((1, width), 1) % slots).astype(f32)
        limits = []
        for i in range(2):
            limit = jnp.where(line[:, 0:1] + first == own_row, offsets[i], 63.0) + 1.0
            limit = jnp.where(members[i] > 0.5, limit, 0.0)
            limits.append(jnp.sum(jnp.where(chosen, limit, 0.0), axis=0, keepdims=True))
        lane = iota((1, width), 1)
        place = lane // (halves * slots) * PIECE
        if halves == 2:
            place = place + lane // slots % 2 * 2
        for k in range(width // step):
            rows = slice(k * step, (k + 1) * step)
            for r in range(PIECE // halves):
                half, parity = r // 2, r % 2
                at = half * WIDTH + parity * DL
                columns = slice(at, at + DL)
                turn = half * WIDTH + 2 * DL
                block = product(
                    padded[parity],
                    jnp.concatenate([ref[rows, columns], ref[rows, turn : turn + 128]], axis=1),
                )
                keep(
                    block,
                    (place[:, rows] + r).astype(f32),
                    [limit[:, rows] for limit in limits],
                    [(ref, rows, columns)],
                )

    highest = jnp.max(jnp.concatenate(tops, axis=0), axis=1, keepdims=True)
    norm = jnp.zeros((2 * HEADS, 128), f32)
    state[0] = jnp.broadcast_to(highest, (2 * HEADS, 128))
    state[1] = attend_sum(scores, sets, highest, norm, total, True)

    tiles = [
        far_ref[p * FAR[2] : p * FAR[2] + 16, KV_COLS:].astype(f32)
        for p in range(PLANE)
    ]
    group = iota((16, 128), 1) // 32
    for c in range(4):
        for m in range(4):
            mixed = tiles[4 * m]
            for k in range(4):
                tile = tiles[4 * m + k]
                if k != c:
                    tile = pltpu.roll(tile, (k - c) * 32 % 128, 1)
                mixed = tile if k == 0 else jnp.where(group == k, tile, mixed)
            turned[(c * 4 + m) * 16 : (c * 4 + m + 1) * 16, :] = mixed
            for t in range(8):
                at = (t * 4 + c) * 512 + m * 128
                index_ref[:, at : at + 128] = turned[
                    pl.ds((c * 4 + m) * 16 + t, 2, stride=8), :
                ].astype(bf16)


def column_kernel(q_ref, ids_ref, before, state, *refs):
    count = len(AWAYS)
    mine, crossed, (out_ref, scores, total) = refs[:count], refs[count], refs[count + 1 :]
    ctx, own_block, offsets, padded, sets, tops, keep = attend_start(q_ref, scores)
    ids = ids_ref[...]
    count = 16 * len(AWAYS)
    line = iota((count, 128), 0)
    lane = iota((count, 128), 1)
    named = jnp.zeros((count, 128), f32)
    shard = ids // 8
    away = (shard // 2 - ctx // 2 + LEVELS) % LEVELS
    turn = jnp.where(away < 3, away, jnp.where(away > 13, away - 11, -8))
    place = (turn * 2 + (shard + ctx) % 2) * 8 + ids % 8
    own_away = (own_block // 16 - ctx // 2 + LEVELS) % LEVELS
    own_turn = jnp.where(own_away < 3, own_away, jnp.where(own_away > 13, own_away - 11, -8))
    own_place = (own_turn * 2 + (own_block // 8 + ctx) % 2) * 8 + own_block % 8
    for i in range(2):
        hit = jnp.where(place[i : i + 1] == iota((count, ids.shape[1]), 0), 1.0, 0.0)
        named = jnp.where(lane == i, jnp.max(hit, axis=1, keepdims=True), named)
    members = named
    named = jnp.maximum(named[:, 0:1], named[:, 1:2])
    code = slot_codes((0, count, 2), jnp.broadcast_to(named, (count, 128)))
    chosen = code == (lane // 32 % 2).astype(f32)
    limits = []
    for i in range(2):
        limit = jnp.where(line[:, 0:1] == own_place, offsets[i], 63.0) + 1.0
        limit = jnp.where(members[:, i : i + 1] > 0.5, limit, 0.0)
        limits.append(jnp.where(chosen, limit, 0.0))
    low = iota((1, 128), 1) < 64
    shown = [
        [
            jnp.where(
                low,
                jnp.sum(limit[n * 8 : (n + 1) * 8], axis=0, keepdims=True),
                jnp.sum(limit[(n + 1) * 8 : (n + 2) * 8], axis=0, keepdims=True),
            )
            for n in range(0, 2 * len(AWAYS), 2)
        ]
        for limit in limits
    ]
    here = iota((1, 128), 1) % 32
    direct = []
    for n in range(len(AWAYS)):
        direct += [(mine[n], slice(0, 64)), (crossed, slice(n * 64, (n + 1) * 64))]
    for first, last in ((0, 2), (2, 4), (4, 5)):
        parts = direct[2 * first : 2 * last]
        turns = [ref[rows, 2 * DL : 2 * DL + 128] for ref, rows in parts]
        for parity in range(2):
            columns = slice(parity * DL, (parity + 1) * DL)
            values = [ref[rows, columns] for ref, rows in parts]
            both = [jnp.concatenate(pair, axis=1) for pair in zip(values, turns)]
            keep(
                product(padded[parity], jnp.concatenate(both, axis=0)),
                jnp.concatenate([(here + 32 * parity).astype(f32)] * (last - first), axis=1),
                [jnp.concatenate(each[first:last], axis=1) for each in shown],
                [(ref, rows, columns) for ref, rows in parts],
            )

    highest = jnp.max(jnp.concatenate(tops, axis=0), axis=1, keepdims=True)
    highest = jnp.maximum(highest, state[0][:, 0:1])
    fade = jnp.exp((state[0] - highest) * score_scale)
    for k in range(4):
        total[k] = before[k] * fade
    norm = attend_sum(scores, sets, highest, state[1] * fade, total, False)
    share = 1.0 / jnp.sum(norm, axis=1, keepdims=True)
    for k in range(4):
        total[k] = total[k] * share
    for h in range(HEADS):
        for k in range(4):
            at = h * DL + k * 128
            out_ref[:, at : at + 128] = total[k, pl.ds(h, 2, stride=HEADS), :].astype(bf16)


def attend_plane(query, ids, near, far):
    return pl.pallas_call(
        plane_kernel,
        out_shape=(
            jax.ShapeDtypeStruct((4, 2 * HEADS, 128), f32),
            jax.ShapeDtypeStruct((2, 2 * HEADS, 128), f32),
            jax.ShapeDtypeStruct((2, 16384), bf16),
        ),
        in_specs=[whole()] * 4,
        out_specs=(whole(),) * 3,
        scratch_shapes=[
            pltpu.VMEM((2 * HEADS, 2816), f32),
            pltpu.VMEM((256, 128), f32),
        ],
        compiler_params=params(),
        cost_estimate=pl.CostEstimate(
            flops=2 * 256 * 2816 * 1152, bytes_accessed=4_000_000, transcendentals=256 * 2816
        ),
        name="attend_plane",
    )(query, ids, near, far)


def attend_column(query, ids, before, state, mine, crossed):
    return pl.pallas_call(
        column_kernel,
        out_shape=jax.ShapeDtypeStruct((2, HEADS * DL), bf16),
        in_specs=[whole()] * (5 + len(mine)),
        out_specs=whole(),
        scratch_shapes=[
            pltpu.VMEM((2 * HEADS, 1280), f32),
            pltpu.VMEM((4, 2 * HEADS, 128), f32),
        ],
        compiler_params=params(),
        cost_estimate=pl.CostEstimate(
            flops=2 * 256 * 1280 * 1152, bytes_accessed=3_000_000, transcendentals=256 * 1280
        ),
        name="attend_column",
    )(query, ids, before, state, *mine, crossed)


def two_levels_on(value):
    pairs = [
        ((level + (2, -2)[core]) % LEVELS * 2 + core, level * 2 + core)
        for level in range(LEVELS)
        for core in range(2)
    ]
    return lax.ppermute(value, "ctx", pairs)


def tie_kernel(value_ref, after_ref, out_ref):
    pass


def tie(value, after):
    return pl.pallas_call(
        tie_kernel,
        out_shape=jax.ShapeDtypeStruct(value.shape, value.dtype),
        in_specs=[anywhere(), anywhere()],
        out_specs=anywhere(),
        input_output_aliases={0: 0},
        name="tie",
    )(value, after)


def join_kernel(*refs):
    out_ref = refs[-1]
    for n, ref in enumerate(refs[:-1]):
        out_ref[n * 64 : (n + 1) * 64, :] = ref[64:, :]


def join(parts):
    return pl.pallas_call(
        join_kernel,
        out_shape=jax.ShapeDtypeStruct((len(parts) * 64, WIDTH), bf16),
        in_specs=[whole()] * len(parts),
        out_specs=whole(),
        compiler_params=params(),
        cost_estimate=pl.CostEstimate(flops=0, bytes_accessed=2_000_000, transcendentals=0),
        name="join",
    )(*parts)


def level_from(value, away):
    pairs = [
        ((level + away) % LEVELS * 2 + core, level * 2 + core)
        for level in range(LEVELS)
        for core in range(2)
    ]
    return lax.ppermute(value, "ctx", pairs)


def swap(value):
    return lax.ppermute(value, "ctx", [(at, at ^ 1) for at in range(2 * LEVELS)])


def exchange(rows):
    parts = rows.reshape(PLANE, rows.shape[0] // PLANE, rows.shape[1])
    got = lax.all_to_all(parts, "pb", split_axis=0, concat_axis=0, tiled=True)
    return got.reshape(rows.shape)


def outer_levels(chunks):
    groups = [
        [(outer * 4 + inner) * 2 + core for outer in range(4)]
        for inner in range(4)
        for core in range(2)
    ]
    got = lax.all_to_all(
        chunks, "ctx", split_axis=0, concat_axis=0, axis_index_groups=groups, tiled=True
    )
    return got.reshape(chunks.shape[0] * chunks.shape[1], chunks.shape[2])


def local(q_latent, kv_cache, index_queries, index_weights, index_keys, q_blocks):
    kv_turned = kv_cache.T
    z, y = pack(kv_turned, index_keys, index_queries, index_weights, q_blocks)
    held = outer_levels(z)
    y = lax.all_to_all(y, "pb", split_axis=0, concat_axis=0, tiled=True)
    across = swap(held)
    others = [level_from(held, 1), level_from(held, 15), two_levels_on(held)]
    near = exchange(gather("near", NEAR, [held, across], y, others))
    swapped = [swap(other) for other in others]
    tables = [held] + others + [across] + swapped
    scores, asked = score(tables, y)
    sent = gather("far", FAR, others + swapped, y, [], scores)
    served = serve(kv_turned, asked, sent)
    far = exchange(tie(sent, near))
    got = {0: served[0]}
    for away in (2, 14, 1, 15):
        got[away] = level_from(served[AWAYS.index(-away % LEVELS)], away)
    mine = [got[away] for away in AWAYS]
    crossed = swap(join(mine))
    query = q_latent.reshape(2, HEADS, DQK)
    before, state, scores = attend_plane(query, q_blocks, near, far)
    return (attend_column(query, q_blocks, before, state, mine, crossed), scores)


def solution(mesh):
    in_specs = (
        P(("ctx", "pb"), None),
        P("ctx", None),
        P(("ctx", "pb"), None),
        P(("ctx", "pb"), None),
        P(("ctx", "pb"), None),
        P(("ctx", "pb"), None),
    )
    out_specs = (P(("ctx", "pb"), None), P(("ctx", "pb"), None))
    return jax.shard_map(local, mesh=mesh, in_specs=in_specs, out_specs=out_specs, check_vma=False)
```
